512 devices in a mesh: tm: 32 (over z, core), panel: 16 (over y, x).
Axes of the slice: x: 4, y: 4, z: 16, core: 2. Of those that a mesh axis runs over, the one named last changes fastest.
Arguments:
- kept_block: float32 [32, 1024, 1024], P('tm', 'panel'), may hold values from -6 to 6
- coupling_in: bfloat16 [32, 1024, 1024], P('tm', None, 'panel'), may hold values from -0.375 to 0.375
- coupling_out: bfloat16 [32, 1024, 1024], P('tm', 'panel'), may hold values from -0.375 to 0.375
- factor: bfloat16 [32, 1024, 1024], P('tm', 'panel'), may hold values from -0.1875 to 0.1875
- source_kept: bfloat16 [32, 1024, 1024], P('tm', 'panel'), may hold values from -6 to 6
- source_odd: bfloat16 [32, 1024, 1024], P('tm', 'panel'), may hold values from -6 to 6
- observed: int32 [32, 1024], P('tm', 'panel'), may hold values 0 or 1
Outputs:
- reduced_block: float32 [32, 1024, 1024], P('tm', 'panel')
- reduced_coupling: float32 [32, 1024, 1024], P('tm', 'panel')
- reduced_source: float32 [32, 1024, 1024], P('tm', 'panel')
The draws below stay inside these ranges and needn't reach their ends.
All inputs are finite; a program needn't handle non-finite values. No bound on the sum of `observed` on one device may be relied on, other than what follows from the above.
Results may differ from the reference program's by a relative error of at most 0.0029.
Values may be sent and summed in bfloat16 or wider, within the bound.
A program may use at most 64 MiB of HBM per device.

```python
import jax
import jax.numpy as jnp
from jax import lax

NODES = 1024
DRAWS = 1024
KEPT = 32


def with_ends(values, own_key, smallest, top_value):
    extent = values.shape
    index_at = [jax.random.randint(jax.random.fold_in(own_key, axis), (), 0, extent[axis]) for axis in range(len(extent))]
    values = values.at[tuple(index_at)].set(smallest)
    longest = extent.index(max(extent))
    index_at[longest] = (index_at[longest] + 1) % extent[longest]
    return values.at[tuple(index_at)].set(top_value)


def block_levels(key, extent, split, smallest, largest):
    loudness = 1.0
    for dim, blocks in split:
        draws = jax.random.uniform(jax.random.fold_in(jax.random.fold_in(key, 6), dim), (blocks,), jnp.float32, smallest / len(split), largest / len(split))
        loudness = loudness * jnp.repeat(jnp.exp(draws), extent[dim] // blocks).reshape((-1,) + (1,) * (len(extent) - 1 - dim))
    return loudness


def scatter_about(own_key, dims, scale, reach, pieces=(), kind=jnp.bfloat16):
    drawn = jax.random.normal(own_key, dims, jnp.float32) * scale
    if len(pieces) > 0:
        drawn = block_levels(own_key, dims, pieces, -0.22, 0.18) * drawn
    return jnp.clip(drawn, min=-reach, max=reach).astype(kind)


def setup_inputs(seed: int = 0) -> dict:
    key_list = jax.random.split(jax.random.key(seed), 8)
    return {
        "kept_block": scatter_about(key_list[0], (KEPT, NODES, NODES), 1.0, 6.0, ((0, 32), (1, 16)), jnp.float32),
        "coupling_in": scatter_about(key_list[1], (KEPT, NODES, NODES), (NODES // 4) ** -0.5, 0.375, ((0, 32), (2, 16))),
        "coupling_out": scatter_about(key_list[2], (KEPT, NODES, NODES), (NODES // 4) ** -0.5, 0.375, ((0, 32), (1, 16))),
        "factor": scatter_about(key_list[3], (KEPT, NODES, NODES), NODES ** -0.5, 0.1875, ((0, 32), (1, 16))),
        "source_kept": scatter_about(key_list[4], (KEPT, NODES, DRAWS), 1.0, 6.0, ((0, 32), (1, 16))),
        "source_odd": scatter_about(key_list[5], (KEPT, NODES, DRAWS), 1.0, 6.0, ((0, 32), (1, 16))),
        "observed": with_ends((jax.random.randint(key_list[6], (KEPT, NODES), 0, 2) < 1).astype(jnp.int32), jax.random.fold_in(key_list[6], 1), 0, 1),
    }


obs_precision = 2.0


def cross_product(left, right):
    return lax.dot_general(left, right, (((0,), (0,)), ((), ())), preferred_element_type=jnp.float32)


def odd_terms(inputs):
    factor_one, couple_in, couple_out, source_one = inputs
    whitened_in = jnp.dot(factor_one, couple_in, preferred_element_type=jnp.float32).astype(jnp.bfloat16)
    whitened_out = jnp.dot(factor_one, couple_out.T, preferred_element_type=jnp.float32).astype(jnp.bfloat16)
    whitened_src = jnp.dot(factor_one, source_one, preferred_element_type=jnp.float32).astype(jnp.bfloat16)
    return whitened_in, whitened_out, whitened_src


def kept_terms(inputs):
    block, whitened_in, whitened_out, whitened_src, partner, partner_src, source_one, mask_one = inputs
    identity = jnp.eye(NODES, dtype=jnp.float32)
    new_block = block + obs_precision * identity * mask_one.astype(jnp.float32)[:, None]
    new_block = new_block - cross_product(partner, partner) - cross_product(whitened_in, whitened_in)
    new_coupling = -cross_product(whitened_out, whitened_in)
    new_source = source_one.astype(jnp.float32) - cross_product(partner, partner_src) - cross_product(whitened_in, whitened_src)
    return new_block, new_coupling, new_source


def reference(kept_block, coupling_in, coupling_out, factor, source_kept, source_odd, observed):
    whitened_in, whitened_out, whitened_src = lax.map(odd_terms, (factor, coupling_in, coupling_out, source_odd))
    partner = jnp.concatenate([jnp.zeros_like(whitened_out[:1]), whitened_out[:-1]], axis=0)
    partner_src = jnp.concatenate([jnp.zeros_like(whitened_src[:1]), whitened_src[:-1]], axis=0)
    reduced_block, reduced_coupling, reduced_source = lax.map(
        kept_terms, (kept_block, whitened_in, whitened_out, whitened_src, partner, partner_src, source_kept, observed))
    return reduced_block, reduced_coupling, reduced_source
```

```python
import jax
import jax.numpy as jnp
from jax import lax
from jax.experimental import pallas as pl
from jax.experimental.pallas import tpu as pltpu
from jax.sharding import PartitionSpec as P

MESH = pl.DeviceIdType.MESH
ROWS = 64
N = 1024
KEYS = (
    "a_R", "a_L", "b_Y",
    "fa_R", "fa_L", "ya_0", "ya_L", "ya_R", "b_R", "b_L", "pb_R", "pb_L",
    "fb_R", "fpb_R", "fb_L", "fpb_L", "ya_2",
    "sib_0", "sib_1",
)
NKEYS = len(KEYS)
SWAP0 = 4 * NKEYS
RET0 = SWAP0 + 4
NSEM = RET0 + 16


def nt(left, right):
    return lax.dot_general(left, right, (((1,), (1,)), ((), ())), preferred_element_type=jnp.float32)


def nn(left, right):
    return jnp.dot(left, right, preferred_element_type=jnp.float32)


def kernel(
    kept_ref, cin_ref, cout_ref, w_ref, sk_ref, s_ref, obs_ref,
    block_ref, coup_ref, src_ref,
    fw, fs, fi, fo, cinv, cint, keptv, skv, obsv, cc, xt, vacc, vb, r13, r45,
    send1, send3, send4, send2, send5, recv1, recv3, recv4, recv2, recv5,
    ssem, rsem, lsem,
):
    kept_n = lax.axis_size("tm")
    k = lax.axis_index("tm")
    panel = lax.axis_index("panel")
    x, y = lax.rem(panel, 4), panel // 4
    core = lax.rem(k, 2)
    half = y // 2
    home = core == half
    guest = core != half
    py = jnp.where(home, y, 3 - y)
    pyq = py + 1 - 2 * lax.rem(py, 2)
    job = k - core + half
    mine = py * 4 + x

    right = {"panel": y * 4 + lax.rem(x + 1, 4)}
    left = {"panel": y * 4 + lax.rem(x + 3, 4)}
    across = {"panel": (y + 1 - 2 * lax.rem(y, 2)) * 4 + x}
    sibling = {"tm": k + 1 - 2 * core}
    partner = {"tm": k + 1 - 2 * core, "panel": (3 - y) * 4 + x}
    follower = {"tm": lax.rem(job + 1, kept_n), "panel": mine}
    has_follower = job + 1 < kept_n
    has_leader = k > 0
    before = jnp.maximum(k - 1, 0)
    before_core = lax.rem(before, 2)
    before_home = before_core == half
    leader = {
        "tm": jnp.where(before_home, before, before + 1 - 2 * before_core),
        "panel": jnp.where(before_home, panel, (3 - y) * 4 + x),
    }

    load_cin = pltpu.make_async_copy(cin_ref.at[0], cinv, lsem.at[0])
    load_kept = pltpu.make_async_copy(kept_ref.at[0], keptv, lsem.at[1])
    load_sk = pltpu.make_async_copy(sk_ref.at[0], skv, lsem.at[2])
    load_obs = pltpu.make_async_copy(obs_ref, obsv, lsem.at[3])
    load_cin.start()

    barrier = pltpu.get_barrier_semaphore()
    for peer in (right, left, across, sibling):
        pl.semaphore_signal(barrier, inc=1, device_id=peer, device_id_type=MESH)

    @pl.when(guest)
    def _():
        pl.semaphore_signal(barrier, inc=1, device_id=partner, device_id_type=MESH)

    @pl.when(has_leader)
    def _():
        pl.semaphore_signal(barrier, inc=1, device_id=leader, device_id_type=MESH)

    full = (fw, fs, fi, fo)
    own = (w_ref.at[0], s_ref.at[0], cint, cout_ref.at[0])

    def rows(m, p, r0, n):
        return full[m].at[pl.ds(pl.multiple_of(p * ROWS + r0, 16), n)]

    def home_copy(m):
        return pltpu.make_async_copy(own[m], rows(m, panel, 0, ROWS), lsem.at[4 + m])

    def guest_copy(m):
        return pltpu.make_async_remote_copy(
            src_ref=own[m], dst_ref=rows(m, panel, 0, ROWS),
            send_sem=ssem.at[SWAP0 + m], recv_sem=rsem.at[SWAP0 + m],
            device_id=partner, device_id_type=MESH,
        )

    @pl.when(home)
    def _():
        for m in (0, 1, 3):
            home_copy(m).start()

    load_cin.wait()
    cint[...] = cinv[...].T
    load_kept.start()
    load_sk.start()
    load_obs.start()

    @pl.when(k == 0)
    def _():
        recv2[...] = jnp.zeros_like(recv2)
        recv5[...] = jnp.zeros_like(recv5)

    @pl.when(home)
    def _():
        home_copy(2).start()

    pl.semaphore_wait(barrier, 4 + guest.astype(jnp.int32) + has_follower.astype(jnp.int32))

    @pl.when(guest)
    def _():
        for m in range(4):
            guest_copy(m).start()

    def swapped(m):
        @pl.when(home)
        def _():
            home_copy(m).wait()

        @pl.when(guest)
        def _():
            guest_copy(m).wait_recv()

    copies = {}

    def send(m, key, p, r0, n, peer):
        at = m * NKEYS + KEYS.index(key)
        copy = pltpu.make_async_remote_copy(
            src_ref=rows(m, p, r0, n), dst_ref=rows(m, p, r0, n),
            send_sem=ssem.at[at], recv_sem=rsem.at[at],
            device_id=peer, device_id_type=MESH,
        )
        copy.start()
        copies[m, key] = copy

    def got(m, *keys):
        for key in keys:
            copies[m, key].wait_recv()

    xl, xr, xo = lax.rem(x + 3, 4), lax.rem(x + 1, 4), lax.rem(x + 2, 4)
    row, rowq = py * 4, pyq * 4

    def s1(m):
        swapped(m)
        send(m, "a_R", mine, 0, 32, right)
        send(m, "a_L", mine, 0, 32, left)
        send(m, "b_Y", mine, 32, 32, across)

    def s2(m):
        got(m, "a_R")
        send(m, "fa_R", row + xl, 0, 16, right)
        got(m, "a_L")
        send(m, "fa_L", row + xr, 16, 16, left)
        send(m, "ya_0", mine, 0, 32, across)
        send(m, "b_R", mine, 32, 32, right)
        send(m, "b_L", mine, 32, 32, left)
        send(m, "ya_L", row + xl, 0, 32, across)
        send(m, "ya_R", row + xr, 0, 32, across)
        got(m, "b_Y")
        send(m, "pb_R", rowq + x, 32, 32, right)
        send(m, "pb_L", rowq + x, 32, 32, left)

    def s3(m):
        got(m, "fa_R", "fa_L")
        send(m, "ya_2", row + xo, 0, 32, across)
        got(m, "b_R")
        send(m, "fb_R", row + xl, 32, 16, right)
        got(m, "b_L")
        send(m, "fb_L", row + xr, 48, 16, left)
        got(m, "pb_R")
        send(m, "fpb_R", rowq + xl, 32, 16, right)
        got(m, "pb_L")
        send(m, "fpb_L", rowq + xr, 48, 16, left)

    def s4(m):
        got(m, "fb_R", "fb_L")
        send(m, "sib_0", row, 0, 4 * ROWS, sibling)
        got(m, "ya_0", "ya_L", "ya_R", "fpb_R", "fpb_L", "ya_2")
        send(m, "sib_1", rowq, 0, 4 * ROWS, sibling)

    def s5(m):
        got(m, "sib_0", "sib_1")

    def back(at, src, dst, peer):
        return pltpu.make_async_remote_copy(
            src_ref=src, dst_ref=dst, send_sem=ssem.at[RET0 + at], recv_sem=rsem.at[RET0 + at],
            device_id=peer, device_id_type=MESH,
        )

    ret4 = back(0, send4, recv4, partner)
    ret5 = back(1, send5, recv5, follower)
    cols = [pl.ds(256 * i, 256) for i in range(4)]
    ret1 = [back(2 + i, send1.at[:, cols[i]], recv1.at[:, cols[i]], partner) for i in range(4)]
    ret3 = [back(6 + i, send3.at[:, cols[i]], recv3.at[:, cols[i]], partner) for i in range(4)]
    ret2 = [back(10 + i, send2.at[:, cols[i]], recv2.at[:, cols[i]], follower) for i in range(4)]

    s1(0)
    s1(1)
    s1(2)
    s2(0)
    s1(3)
    s2(1)
    s3(0)
    s2(2)
    s3(1)
    s4(0)
    s2(3)
    cc[0:ROWS, :] = fi[pl.ds(pl.multiple_of(mine * ROWS, ROWS), ROWS), :]
    cc[ROWS:, :] = fo[pl.ds(pl.multiple_of(mine * ROWS, ROWS), ROWS), :]
    s5(0)
    for i in range(4):
        part = fw[cols[i], :]
        xt[...] = nt(cc[...], part).astype(jnp.bfloat16)
        if i == 0:
            vacc[...] = nn(xt[...], part)
        else:
            vacc[...] += nn(xt[...], part)
    vb[...] = vacc[...].astype(jnp.bfloat16)
    s3(2)
    s4(1)
    s3(3)
    s5(1)
    for i in range(4):
        part = nn(vb[:, cols[i]], fs[cols[i], :])
        if i == 0:
            r45[...] = part
        else:
            r45[...] += part
    send5[...] = r45[ROWS:, :].astype(jnp.bfloat16)

    @pl.when(has_follower)
    def _():
        ret5.start()

    @pl.when(guest)
    def _():
        send4[...] = r45[:ROWS, :].astype(jnp.bfloat16)
        ret4.start()

    s4(2)
    s5(2)
    for i in range(4):
        r13[:, cols[i]] = nt(vb[...], fi[cols[i], :])

        @pl.when(guest)
        def _():
            send1[:, cols[i]] = r13[:ROWS, cols[i]].astype(jnp.bfloat16)
            send3[:, cols[i]] = r13[ROWS:, cols[i]].astype(jnp.bfloat16)
            ret1[i].start()
            ret3[i].start()

    s4(3)
    s5(3)
    for i in range(4):
        send2[:, cols[i]] = nt(vb[ROWS:, :], fo[cols[i], :]).astype(jnp.bfloat16)

        @pl.when(has_follower)
        def _():
            ret2[i].start()

    load_kept.wait()
    load_sk.wait()
    load_obs.wait()

    @pl.when(has_leader)
    def _():
        ret5.wait_recv()

    @pl.when(home)
    def _():
        src_ref[0] = skv[...].astype(jnp.float32) - recv5[...].astype(jnp.float32) - r45[:ROWS, :]
        coup_ref[0] = -r13[ROWS:, :]
        keptv[...] = keptv[...] - r13[:ROWS, :]

    @pl.when(guest)
    def _():
        ret4.wait_recv()
        src_ref[0] = (
            skv[...].astype(jnp.float32) - recv5[...].astype(jnp.float32) - recv4[...].astype(jnp.float32)
        )
        for i in range(4):
            ret3[i].wait_recv()
        coup_ref[0] = -recv3[...].astype(jnp.float32)
        for i in range(4):
            ret1[i].wait_recv()
        keptv[...] = keptv[...] - recv1[...].astype(jnp.float32)

    at = pl.ds(pl.multiple_of(panel // 2 * 128, 128), 128)
    twice = 2.0 * obsv[...].astype(jnp.float32)
    twice = jnp.concatenate([twice, twice], axis=1)
    on = lax.broadcasted_iota(jnp.int32, (ROWS, 128), 1) == (
        lax.broadcasted_iota(jnp.int32, (ROWS, 128), 0) + ROWS * lax.rem(panel, 2)
    )
    keptv[:, at] = keptv[:, at] + jnp.where(on, jnp.broadcast_to(twice, (ROWS, 128)), 0.0)

    @pl.when(has_leader)
    def _():
        for i in range(4):
            ret2[i].wait_recv()

    block_ref[0] = keptv[...] - recv2[...].astype(jnp.float32)

    for copy in copies.values():
        copy.wait_send()

    @pl.when(guest)
    def _():
        for m in range(4):
            guest_copy(m).wait_send()
        ret4.wait_send()
        for i in range(4):
            ret1[i].wait_send()
            ret3[i].wait_send()

    @pl.when(has_follower)
    def _():
        ret5.wait_send()
        for i in range(4):
            ret2[i].wait_send()


def body(*args):
    bf16, f32 = jnp.bfloat16, jnp.float32
    vmem = pltpu.VMEM
    wide = lambda rows, dtype: vmem((rows, N), dtype)
    return pl.pallas_call(
        kernel,
        out_shape=tuple(jax.ShapeDtypeStruct((1, ROWS, N), f32) for _ in range(3)),
        in_specs=[pl.BlockSpec(memory_space=pl.ANY)] * 7,
        out_specs=(pl.BlockSpec(memory_space=pltpu.VMEM),) * 3,
        scratch_shapes=[wide(N, bf16)] * 4
        + [vmem((N, ROWS), bf16), wide(ROWS, bf16), wide(ROWS, f32), wide(ROWS, bf16), vmem((1, ROWS), jnp.int32)]
        + [wide(2 * ROWS, bf16), vmem((2 * ROWS, 256), bf16), wide(2 * ROWS, f32), wide(2 * ROWS, bf16)]
        + [wide(2 * ROWS, f32)] * 2
        + [wide(ROWS, bf16)] * 10
        + [pltpu.SemaphoreType.DMA((NSEM,))] * 2
        + [pltpu.SemaphoreType.DMA((8,))],
        compiler_params=pltpu.CompilerParams(
            collective_id=0, has_side_effects=True, vmem_limit_bytes=40 << 20
        ),
    )(*args)


def solution(mesh):
    return jax.shard_map(
        body,
        mesh=mesh,
        in_specs=(
            P("tm", "panel", None),
            P("tm", None, "panel"),
            P("tm", "panel", None),
            P("tm", "panel", None),
            P("tm", "panel", None),
            P("tm", "panel", None),
            P("tm", "panel"),
        ),
        out_specs=(P("tm", "panel", None), P("tm", "panel", None), P("tm", "panel", None)),
        check_vma=False,
    )
```

```python
import jax
import jax.numpy as jnp
from jax import lax
from jax.experimental import pallas as pl
from jax.experimental.pallas import tpu as pltpu
from jax.sharding import PartitionSpec as P

MESH = pl.DeviceIdType.MESH
ROWS = 64
N = 1024
KEYS = (
    "a_R", "a_L", "b_Y",
    "fa_R", "fa_L", "ya_0", "ya_L", "ya_R", "b_R", "b_L", "pb_R", "pb_L",
    "fb_R", "fpb_R", "fb_L", "fpb_L", "ya_2",
    "sib_0", "sib_1",
)
NKEYS = len(KEYS)
SWAP0 = 4 * NKEYS
RET0 = SWAP0 + 4
NSEM = RET0 + 16


def nt(left, right):
    return lax.dot_general(left, right, (((1,), (1,)), ((), ())), preferred_element_type=jnp.float32)


def nn(left, right):
    return jnp.dot(left, right, preferred_element_type=jnp.float32)


def kernel(
    kept_ref, cin_ref, cout_ref, w_ref, sk_ref, s_ref, obs_ref,
    block_ref, coup_ref, src_ref,
    fw, fs, fi, fo, keptv, skv, obsv, cc, xt, vacc, vb, r13, r45,
    send1, send3, send4, send2, send5, recv1, recv3, recv4, recv2, recv5,
    ssem, rsem, lsem,
):
    kept_n = lax.axis_size("tm")
    k = lax.axis_index("tm")
    panel = lax.axis_index("panel")
    x, y = lax.rem(panel, 4), panel // 4
    core = lax.rem(k, 2)
    half = y // 2
    home = core == half
    guest = core != half
    py = jnp.where(home, y, 3 - y)
    pyq = py + 1 - 2 * lax.rem(py, 2)
    job = k - core + half
    mine = py * 4 + x

    right = {"panel": y * 4 + lax.rem(x + 1, 4)}
    left = {"panel": y * 4 + lax.rem(x + 3, 4)}
    across = {"panel": (y + 1 - 2 * lax.rem(y, 2)) * 4 + x}
    sibling = {"tm": k + 1 - 2 * core}
    partner = {"tm": k + 1 - 2 * core, "panel": (3 - y) * 4 + x}
    follower = {"tm": lax.rem(job + 1, kept_n), "panel": mine}
    has_follower = job + 1 < kept_n
    has_leader = k > 0
    before = jnp.maximum(k - 1, 0)
    before_core = lax.rem(before, 2)
    before_home = before_core == half
    leader = {
        "tm": jnp.where(before_home, before, before + 1 - 2 * before_core),
        "panel": jnp.where(before_home, panel, (3 - y) * 4 + x),
    }

    load_kept = pltpu.make_async_copy(kept_ref.at[0], keptv, lsem.at[1])
    load_sk = pltpu.make_async_copy(sk_ref.at[0], skv, lsem.at[2])
    load_obs = pltpu.make_async_copy(obs_ref, obsv, lsem.at[3])

    barrier = pltpu.get_barrier_semaphore()
    for peer in (right, left, across, sibling):
        pl.semaphore_signal(barrier, inc=1, device_id=peer, device_id_type=MESH)

    @pl.when(guest)
    def _():
        pl.semaphore_signal(barrier, inc=1, device_id=partner, device_id_type=MESH)

    @pl.when(has_leader)
    def _():
        pl.semaphore_signal(barrier, inc=1, device_id=leader, device_id_type=MESH)

    full = (fw, fs, fi, fo)
    own = (w_ref.at[0], s_ref.at[0], cin_ref.at[0], cout_ref.at[0])

    def rows(m, p, r0, n):
        return full[m].at[pl.ds(pl.multiple_of(p * ROWS + r0, 16), n)]

    def home_copy(m):
        return pltpu.make_async_copy(own[m], rows(m, panel, 0, ROWS), lsem.at[4 + m])

    def guest_copy(m):
        return pltpu.make_async_remote_copy(
            src_ref=own[m], dst_ref=rows(m, panel, 0, ROWS),
            send_sem=ssem.at[SWAP0 + m], recv_sem=rsem.at[SWAP0 + m],
            device_id=partner, device_id_type=MESH,
        )

    @pl.when(home)
    def _():
        for m in range(4):
            home_copy(m).start()

    load_kept.start()
    load_sk.start()
    load_obs.start()

    @pl.when(k == 0)
    def _():
        recv2[...] = jnp.zeros_like(recv2)
        recv5[...] = jnp.zeros_like(recv5)

    pl.semaphore_wait(barrier, 4 + guest.astype(jnp.int32) + has_follower.astype(jnp.int32))

    @pl.when(guest)
    def _():
        for m in range(4):
            guest_copy(m).start()

    def swapped(m):
        @pl.when(home)
        def _():
            home_copy(m).wait()

        @pl.when(guest)
        def _():
            guest_copy(m).wait_recv()

    copies = {}

    def send(m, key, p, r0, n, peer):
        at = m * NKEYS + KEYS.index(key)
        copy = pltpu.make_async_remote_copy(
            src_ref=rows(m, p, r0, n), dst_ref=rows(m, p, r0, n),
            send_sem=ssem.at[at], recv_sem=rsem.at[at],
            device_id=peer, device_id_type=MESH,
        )
        copy.start()
        copies[m, key] = copy

    def got(m, *keys):
        for key in keys:
            copies[m, key].wait_recv()

    xl, xr, xo = lax.rem(x + 3, 4), lax.rem(x + 1, 4), lax.rem(x + 2, 4)
    row, rowq = py * 4, pyq * 4

    def s1(m):
        swapped(m)
        send(m, "a_R", mine, 0, 32, right)
        send(m, "a_L", mine, 0, 32, left)
        send(m, "b_Y", mine, 32, 32, across)

    def s2(m):
        got(m, "a_R")
        send(m, "fa_R", row + xl, 0, 16, right)
        got(m, "a_L")
        send(m, "fa_L", row + xr, 16, 16, left)
        send(m, "ya_0", mine, 0, 32, across)
        send(m, "b_R", mine, 32, 32, right)
        send(m, "b_L", mine, 32, 32, left)
        send(m, "ya_L", row + xl, 0, 32, across)
        send(m, "ya_R", row + xr, 0, 32, across)
        got(m, "b_Y")
        send(m, "pb_R", rowq + x, 32, 32, right)
        send(m, "pb_L", rowq + x, 32, 32, left)

    def s3(m):
        got(m, "fa_R", "fa_L")
        send(m, "ya_2", row + xo, 0, 32, across)
        got(m, "b_R")
        send(m, "fb_R", row + xl, 32, 16, right)
        got(m, "b_L")
        send(m, "fb_L", row + xr, 48, 16, left)
        got(m, "pb_R")
        send(m, "fpb_R", rowq + xl, 32, 16, right)
        got(m, "pb_L")
        send(m, "fpb_L", rowq + xr, 48, 16, left)

    def s4(m):
        got(m, "fb_R", "fb_L")
        send(m, "sib_0", row, 0, 4 * ROWS, sibling)
        got(m, "ya_0", "ya_L", "ya_R", "fpb_R", "fpb_L", "ya_2")
        send(m, "sib_1", rowq, 0, 4 * ROWS, sibling)

    def s5(m):
        got(m, "sib_0", "sib_1")

    def back(at, src, dst, peer):
        return pltpu.make_async_remote_copy(
            src_ref=src, dst_ref=dst, send_sem=ssem.at[RET0 + at], recv_sem=rsem.at[RET0 + at],
            device_id=peer, device_id_type=MESH,
        )

    ret4 = back(0, send4, recv4, partner)
    ret5 = back(1, send5, recv5, follower)
    cols = [pl.ds(256 * i, 256) for i in range(4)]
    ret1 = [back(2 + i, send1.at[:, cols[i]], recv1.at[:, cols[i]], partner) for i in range(4)]
    ret3 = [back(6 + i, send3.at[:, cols[i]], recv3.at[:, cols[i]], partner) for i in range(4)]
    ret2 = [back(10 + i, send2.at[:, cols[i]], recv2.at[:, cols[i]], follower) for i in range(4)]

    s1(0)
    s1(1)
    s1(2)
    s2(0)
    s1(3)
    s2(1)
    s3(0)
    s2(2)
    s3(1)
    s4(0)
    s2(3)
    cc[0:ROWS, :] = fi[pl.ds(pl.multiple_of(mine * ROWS, ROWS), ROWS), :]
    cc[ROWS:, :] = fo[pl.ds(pl.multiple_of(mine * ROWS, ROWS), ROWS), :]
    s5(0)
    for i in range(4):
        part = fw[cols[i], :]
        xt[...] = nt(cc[...], part).astype(jnp.bfloat16)
        if i == 0:
            vacc[...] = nn(xt[...], part)
        else:
            vacc[...] += nn(xt[...], part)
    vb[...] = vacc[...].astype(jnp.bfloat16)
    s3(2)
    s4(1)
    s3(3)
    s5(1)
    for i in range(4):
        part = nn(vb[:, cols[i]], fs[cols[i], :])
        if i == 0:
            r45[...] = part
        else:
            r45[...] += part
    send5[...] = r45[ROWS:, :].astype(jnp.bfloat16)

    @pl.when(has_follower)
    def _():
        ret5.start()

    @pl.when(guest)
    def _():
        send4[...] = r45[:ROWS, :].astype(jnp.bfloat16)
        ret4.start()

    s4(2)
    s5(2)
    for i in range(4):
        r13[:, cols[i]] = nt(vb[...], fi[cols[i], :])

        @pl.when(guest)
        def _():
            send1[:, cols[i]] = r13[:ROWS, cols[i]].astype(jnp.bfloat16)
            send3[:, cols[i]] = r13[ROWS:, cols[i]].astype(jnp.bfloat16)
            ret1[i].start()
            ret3[i].start()

    s4(3)
    s5(3)
    for i in range(4):
        send2[:, cols[i]] = nt(vb[ROWS:, :], fo[cols[i], :]).astype(jnp.bfloat16)

        @pl.when(has_follower)
        def _():
            ret2[i].start()

    load_kept.wait()
    load_sk.wait()
    load_obs.wait()

    @pl.when(has_leader)
    def _():
        ret5.wait_recv()

    @pl.when(home)
    def _():
        src_ref[0] = skv[...].astype(jnp.float32) - recv5[...].astype(jnp.float32) - r45[:ROWS, :]
        coup_ref[0] = -r13[ROWS:, :]
        keptv[...] = keptv[...] - r13[:ROWS, :]

    @pl.when(guest)
    def _():
        ret4.wait_recv()
        src_ref[0] = (
            skv[...].astype(jnp.float32) - recv5[...].astype(jnp.float32) - recv4[...].astype(jnp.float32)
        )
        for i in range(4):
            ret3[i].wait_recv()
        coup_ref[0] = -recv3[...].astype(jnp.float32)
        for i in range(4):
            ret1[i].wait_recv()
        keptv[...] = keptv[...] - recv1[...].astype(jnp.float32)

    at = pl.ds(pl.multiple_of(panel // 2 * 128, 128), 128)
    twice = 2.0 * obsv[...].astype(jnp.float32)
    twice = jnp.concatenate([twice, twice], axis=1)
    on = lax.broadcasted_iota(jnp.int32, (ROWS, 128), 1) == (
        lax.broadcasted_iota(jnp.int32, (ROWS, 128), 0) + ROWS * lax.rem(panel, 2)
    )
    keptv[:, at] = keptv[:, at] + jnp.where(on, jnp.broadcast_to(twice, (ROWS, 128)), 0.0)

    @pl.when(has_leader)
    def _():
        for i in range(4):
            ret2[i].wait_recv()

    block_ref[0] = keptv[...] - recv2[...].astype(jnp.float32)

    for copy in copies.values():
        copy.wait_send()

    @pl.when(guest)
    def _():
        for m in range(4):
            guest_copy(m).wait_send()
        ret4.wait_send()
        for i in range(4):
            ret1[i].wait_send()
            ret3[i].wait_send()

    @pl.when(has_follower)
    def _():
        ret5.wait_send()
        for i in range(4):
            ret2[i].wait_send()


def store(*refs):
    ins, outs, sem = refs[:3], refs[3:6], refs[6]
    copies = [pltpu.make_async_copy(ins[i], outs[i], sem.at[i]) for i in range(3)]
    for copy in copies:
        copy.start()
    for copy in copies:
        copy.wait()


def body(kept_block, coupling_in, *rest):
    args = (kept_block, jnp.swapaxes(coupling_in, 1, 2), *rest)
    bf16, f32 = jnp.bfloat16, jnp.float32
    vmem = pltpu.VMEM
    wide = lambda rows, dtype: vmem((rows, N), dtype)
    shapes = tuple(jax.ShapeDtypeStruct((1, ROWS, N), f32) for _ in range(3))
    results = pl.pallas_call(
        kernel,
        out_shape=shapes,
        in_specs=[pl.BlockSpec(memory_space=pltpu.HBM)] * 7,
        out_specs=(pl.BlockSpec(memory_space=pltpu.VMEM),) * 3,
        scratch_shapes=[wide(N, bf16)] * 4
        + [wide(ROWS, f32), wide(ROWS, bf16), vmem((1, ROWS), jnp.int32)]
        + [wide(2 * ROWS, bf16), vmem((2 * ROWS, 256), bf16), wide(2 * ROWS, f32), wide(2 * ROWS, bf16)]
        + [wide(2 * ROWS, f32)] * 2
        + [wide(ROWS, bf16)] * 10
        + [pltpu.SemaphoreType.DMA((NSEM,))] * 2
        + [pltpu.SemaphoreType.DMA((8,))],
        compiler_params=pltpu.CompilerParams(
            collective_id=0, has_side_effects=True, vmem_limit_bytes=62 << 20
        ),
    )(*args)
    return pl.pallas_call(
        store,
        out_shape=shapes,
        in_specs=[pl.BlockSpec(memory_space=pltpu.VMEM)] * 3,
        out_specs=(pl.BlockSpec(memory_space=pltpu.HBM),) * 3,
        scratch_shapes=[pltpu.SemaphoreType.DMA((3,))],
    )(*results)


def solution(mesh):
    return jax.shard_map(
        body,
        mesh=mesh,
        in_specs=(
            P("tm", "panel", None),
            P("tm", None, "panel"),
            P("tm", "panel", None),
            P("tm", "panel", None),
            P("tm", "panel", None),
            P("tm", "panel", None),
            P("tm", "panel"),
        ),
        out_specs=(P("tm", "panel", None), P("tm", "panel", None), P("tm", "panel", None)),
        check_vma=False,
    )
```

```python
import jax
import jax.numpy as jnp
from jax import lax
from jax.experimental import pallas as pl
from jax.experimental.pallas import tpu as pltpu
from jax.sharding import PartitionSpec as P

MESH = pl.DeviceIdType.MESH
ROWS = 64
N = 1024
KEYS = (
    "a_R", "a_L", "b_Y",
    "fa_R", "fa_L", "ya_0", "ya_L", "ya_R", "b_R", "b_L", "pb_R", "pb_L",
    "fb_R", "fpb_R", "fb_L", "fpb_L", "ya_2",
    "sib_0", "sib_x", "sib_l", "sib_r", "sib_o",
)
NKEYS = len(KEYS)
SWAP0 = 4 * NKEYS
RET0 = SWAP0 + 4
NSEM = RET0 + 14
SPLIT = ((32, 16, 16),) * 4


SEQ = (('s1', 0), ('s1', 1), ('s1', 2), ('o2', 0), ('s2', 0), ('s1', 3), ('o2', 1), ('s2', 1), ('s3', 0), ('o2', 2), ('s2', 2), ('s3', 1), ('s4a', 0), ('s4b', 0), ('o2', 3), ('s2', 3), ('c0', 0), ('s3', 2), ('s4a', 1), ('s4b', 1), ('c1', 1), ('s3', 3), ('s4a', 2), ('s4b', 2), ('c2', 2))


def nt(left, right):
    return lax.dot_general(left, right, (((1,), (1,)), ((), ())), preferred_element_type=jnp.float32)


def nn(left, right):
    return jnp.dot(left, right, preferred_element_type=jnp.float32)


def kernel(
    kept_ref, cin_ref, cout_ref, w_ref, sk_ref, s_ref, obs_ref,
    block_ref, coup_ref, src_ref,
    fw, fs, fo, fi, keptv, skv, obsv, cc, xt, vacc, vb, r45,
    send1, send3, send4, send2, send5, recv1, recv3, recv4, recv2, recv5,
    ssem, rsem, lsem, ready,
):
    kept_n = lax.axis_size("tm")
    k = lax.axis_index("tm")
    panel = lax.axis_index("panel")
    x, y = lax.rem(panel, 4), panel // 4
    core = lax.rem(k, 2)
    half = y // 2
    home = core == half
    guest = core != half
    py = jnp.where(home, y, 3 - y)
    pyq = py + 1 - 2 * lax.rem(py, 2)
    job = k - core + half
    mine = py * 4 + x

    right = {"panel": y * 4 + lax.rem(x + 1, 4)}
    left = {"panel": y * 4 + lax.rem(x + 3, 4)}
    across = {"panel": (y + 1 - 2 * lax.rem(y, 2)) * 4 + x}
    sibling = {"tm": k + 1 - 2 * core}
    partner = {"tm": k + 1 - 2 * core, "panel": (3 - y) * 4 + x}
    follower = {"tm": lax.rem(job + 1, kept_n), "panel": mine}
    has_follower = job + 1 < kept_n
    has_leader = k > 0
    before = jnp.maximum(k - 1, 0)
    before_core = lax.rem(before, 2)
    before_home = before_core == half
    leader = {
        "tm": jnp.where(before_home, before, before + 1 - 2 * before_core),
        "panel": jnp.where(before_home, panel, (3 - y) * 4 + x),
    }

    load_kept = pltpu.make_async_copy(kept_ref.at[0], keptv, lsem.at[0])
    load_sk = pltpu.make_async_copy(sk_ref.at[0], skv, lsem.at[1])
    load_obs = pltpu.make_async_copy(obs_ref, obsv, lsem.at[2])

    barrier = pltpu.get_barrier_semaphore()
    for peer in (right, left, across, sibling):
        pl.semaphore_signal(barrier, inc=1, device_id=peer, device_id_type=MESH)

    @pl.when(guest)
    def _():
        pl.semaphore_signal(barrier, inc=1, device_id=partner, device_id_type=MESH)

    @pl.when(has_follower)
    def _():
        pl.semaphore_signal(barrier, inc=1, device_id=follower, device_id_type=MESH)

    full = (fw, fs, fo, fi)
    own = (w_ref.at[0], s_ref.at[0], cout_ref.at[0], cin_ref.at[0])

    def rows(m, p, r0, n):
        return full[m].at[pl.ds(pl.multiple_of(p * ROWS + r0, 16), n)]

    def home_copy(m):
        return pltpu.make_async_copy(own[m], rows(m, panel, 0, ROWS), lsem.at[3 + m])

    def guest_copy(m):
        return pltpu.make_async_remote_copy(
            src_ref=own[m], dst_ref=rows(m, panel, 0, ROWS),
            send_sem=ssem.at[SWAP0 + m], recv_sem=rsem.at[SWAP0 + m],
            device_id=partner, device_id_type=MESH,
        )

    @pl.when(home)
    def _():
        for m in range(4):
            home_copy(m).start()

    load_kept.start()
    load_sk.start()
    load_obs.start()

    @pl.when(k == 0)
    def _():
        recv2[...] = jnp.zeros_like(recv2)
        recv5[...] = jnp.zeros_like(recv5)

    pl.semaphore_wait(barrier, 4 + guest.astype(jnp.int32) + has_leader.astype(jnp.int32))

    @pl.when(guest)
    def _():
        for m in range(4):
            guest_copy(m).start()

    @pl.when(has_leader)
    def _():
        pl.semaphore_signal(ready, inc=1, device_id=leader, device_id_type=MESH)

    def swapped(m):
        @pl.when(home)
        def _():
            home_copy(m).wait()

        @pl.when(guest)
        def _():
            guest_copy(m).wait_recv()

    copies = {}

    def send(m, key, p, r0, n, peer):
        if n == 0:
            return
        at = m * NKEYS + KEYS.index(key)
        copy = pltpu.make_async_remote_copy(
            src_ref=rows(m, p, r0, n), dst_ref=rows(m, p, r0, n),
            send_sem=ssem.at[at], recv_sem=rsem.at[at],
            device_id=peer, device_id_type=MESH,
        )
        copy.start()
        copies[m, key] = copy

    def got(m, *keys):
        for key in keys:
            if (m, key) in copies:
                copies[m, key].wait_recv()

    xl, xr, xo = lax.rem(x + 3, 4), lax.rem(x + 1, 4), lax.rem(x + 2, 4)
    row, rowq = py * 4, pyq * 4

    def s1(m):
        a = SPLIT[m][0]
        swapped(m)
        send(m, "a_R", mine, 0, a, right)
        send(m, "a_L", mine, 0, a, left)
        send(m, "b_Y", mine, a, ROWS - a, across)

    def o2(m):
        a = SPLIT[m][0]
        send(m, "ya_0", mine, 0, a, across)
        send(m, "b_R", mine, a, ROWS - a, right)
        send(m, "b_L", mine, a, ROWS - a, left)

    def s2(m):
        a, ra, _ = SPLIT[m]
        got(m, "a_R")
        send(m, "fa_R", row + xl, 0, ra, right)
        got(m, "a_L")
        send(m, "fa_L", row + xr, ra, a - ra, left)
        send(m, "ya_L", row + xl, 0, a, across)
        send(m, "ya_R", row + xr, 0, a, across)
        got(m, "b_Y")
        send(m, "pb_R", rowq + x, a, ROWS - a, right)
        send(m, "pb_L", rowq + x, a, ROWS - a, left)

    def s3(m):
        a, _, rb = SPLIT[m]
        got(m, "fa_R", "fa_L")
        send(m, "ya_2", row + xo, 0, a, across)
        got(m, "b_R")
        send(m, "fb_R", row + xl, a, rb, right)
        got(m, "b_L")
        send(m, "fb_L", row + xr, a + rb, ROWS - a - rb, left)
        got(m, "pb_R")
        send(m, "fpb_R", rowq + xl, a, rb, right)
        got(m, "pb_L")
        send(m, "fpb_L", rowq + xr, a + rb, ROWS - a - rb, left)

    def s4a(m):
        got(m, "fb_R", "fb_L")
        send(m, "sib_0", row, 0, 4 * ROWS, sibling)

    def s4b(m):
        got(m, "ya_0")
        send(m, "sib_x", rowq + x, 0, ROWS, sibling)
        got(m, "ya_L")
        send(m, "sib_l", rowq + xl, 0, ROWS, sibling)
        got(m, "ya_R")
        send(m, "sib_r", rowq + xr, 0, ROWS, sibling)
        got(m, "fpb_R", "fpb_L", "ya_2")
        send(m, "sib_o", rowq + xo, 0, ROWS, sibling)

    def s5(m):
        got(m, "sib_0", "sib_x", "sib_l", "sib_r", "sib_o")

    def back(at, src, dst, peer):
        return pltpu.make_async_remote_copy(
            src_ref=src, dst_ref=dst, send_sem=ssem.at[RET0 + at], recv_sem=rsem.at[RET0 + at],
            device_id=peer, device_id_type=MESH,
        )

    def span(p):
        return pl.ds(pl.multiple_of(p * 256, 256), 256)

    cols = [pl.ds(256 * i, 256) for i in range(4)]
    groups = [span(p) for p in (py, 3 - py, pyq, 3 - pyq)]
    theirs = [span(p) for p in (3 - py, py, 3 - pyq, pyq)]
    ret4 = back(0, send4, recv4, partner)
    ret5 = back(1, send5, recv5, follower)
    ret1 = [back(2 + i, send1.at[:, groups[i]], recv1.at[:, groups[i]], partner) for i in range(4)]
    ret3 = [back(6 + i, send3.at[:, groups[i]], recv3.at[:, groups[i]], partner) for i in range(4)]
    ret2 = [back(10 + i, send2.at[:, cols[i]], recv2.at[:, cols[i]], follower) for i in range(4)]

    def c0(m):
        s5(m)
        cc[0:ROWS, :] = fi[pl.ds(pl.multiple_of(mine * ROWS, ROWS), ROWS), :]
        cc[ROWS:, :] = fo[pl.ds(pl.multiple_of(mine * ROWS, ROWS), ROWS), :]
        for i in range(4):
            part = fw[cols[i], :]
            xt[...] = nt(cc[...], part).astype(jnp.bfloat16)
            if i == 0:
                vacc[...] = nn(xt[...], part)
            else:
                vacc[...] += nn(xt[...], part)
        vb[...] = vacc[...].astype(jnp.bfloat16)

    def c1(m):
        s5(m)
        for i in range(4):
            part = nn(vb[:, cols[i]], fs[cols[i], :])
            if i == 0:
                r45[...] = part
            else:
                r45[...] += part
        send5[...] = r45[ROWS:, :].astype(jnp.bfloat16)

        @pl.when(has_follower)
        def _():
            pl.semaphore_wait(ready, 1)
            ret5.start()

        @pl.when(guest)
        def _():
            send4[...] = r45[:ROWS, :].astype(jnp.bfloat16)
            ret4.start()


    def c2(m):
        s5(m)
        for i in range(4):
            send2[:, cols[i]] = nt(vb[ROWS:, :], fo[cols[i], :]).astype(jnp.bfloat16)

            @pl.when(has_follower)
            def _():
                ret2[i].start()


    for step, m in SEQ:
        {"s1": s1, "o2": o2, "s2": s2, "s3": s3, "s4a": s4a, "s4b": s4b, "c0": c0, "c1": c1, "c2": c2}[step](m)
    s4a(3)
    load_kept.wait()
    load_sk.wait()
    load_obs.wait()
    at = pl.ds(pl.multiple_of(panel // 2 * 128, 128), 128)
    twice = 2.0 * obsv[...].astype(jnp.float32)
    twice = jnp.concatenate([twice, twice], axis=1)
    on = lax.broadcasted_iota(jnp.int32, (ROWS, 128), 1) == (
        lax.broadcasted_iota(jnp.int32, (ROWS, 128), 0) + ROWS * lax.rem(panel, 2)
    )
    keptv[:, at] = keptv[:, at] + jnp.where(on, jnp.broadcast_to(twice, (ROWS, 128)), 0.0)

    @pl.when(has_leader)
    def _():
        ret5.wait_recv()

    @pl.when(home)
    def _():
        src_ref[0] = skv[...].astype(jnp.float32) - recv5[...].astype(jnp.float32) - r45[:ROWS, :]

    @pl.when(guest)
    def _():
        ret4.wait_recv()
        src_ref[0] = skv[...].astype(jnp.float32) - recv5[...].astype(jnp.float32) - recv4[...].astype(jnp.float32)

    s4b(3)

    @pl.when(has_leader)
    def _():
        for i in range(4):
            ret2[i].wait_recv()

    keptv[...] = keptv[...] - recv2[...].astype(jnp.float32)
    for i, keys in enumerate(((), ("sib_0",), (), ("sib_x", "sib_l", "sib_r", "sib_o"))):
        got(3, *keys)
        both = nt(vb[...], fi[groups[i], :])

        @pl.when(home)
        def _():
            block_ref[0, :, groups[i]] = keptv[:, groups[i]] - both[:ROWS, :]
            coup_ref[0, :, groups[i]] = -both[ROWS:, :]

        @pl.when(guest)
        def _():
            send1[:, groups[i]] = both[:ROWS, :].astype(jnp.bfloat16)
            send3[:, groups[i]] = both[ROWS:, :].astype(jnp.bfloat16)
            ret1[i].start()
            ret3[i].start()

    @pl.when(guest)
    def _():
        for i in range(4):
            ret1[i].wait_recv()
            block_ref[0, :, theirs[i]] = keptv[:, theirs[i]] - recv1[:, theirs[i]].astype(jnp.float32)
            ret3[i].wait_recv()
            coup_ref[0, :, theirs[i]] = -recv3[:, theirs[i]].astype(jnp.float32)

    for copy in copies.values():
        copy.wait_send()

    @pl.when(guest)
    def _():
        for m in range(4):
            guest_copy(m).wait_send()
        ret4.wait_send()
        for i in range(4):
            ret1[i].wait_send()
            ret3[i].wait_send()

    @pl.when(has_follower)
    def _():
        ret5.wait_send()
        for i in range(4):
            ret2[i].wait_send()


def store(*refs):
    ins, outs, sem = refs[:3], refs[3:6], refs[6]
    puts = [pltpu.make_async_copy(ins[i], outs[i], sem.at[i]) for i in range(3)]
    for copy in puts:
        copy.start()
    for copy in puts:
        copy.wait()


def body(kept_block, coupling_in, *rest):
    args = (kept_block, jnp.swapaxes(coupling_in, 1, 2), *rest)
    args = tuple(pltpu.with_memory_space_constraint(a, pltpu.HBM) for a in args)
    bf16, f32 = jnp.bfloat16, jnp.float32
    vmem = pltpu.VMEM
    wide = lambda rows, dtype: vmem((rows, N), dtype)
    shapes = tuple(jax.ShapeDtypeStruct((1, ROWS, N), f32) for _ in range(3))
    results = pl.pallas_call(
        kernel,
        out_shape=shapes,
        in_specs=[pl.BlockSpec(memory_space=pltpu.HBM)] * 7,
        out_specs=(pl.BlockSpec(memory_space=pltpu.VMEM),) * 3,
        scratch_shapes=[wide(N, bf16)] * 4
        + [wide(ROWS, f32), wide(ROWS, bf16), vmem((1, ROWS), jnp.int32)]
        + [wide(2 * ROWS, bf16), vmem((2 * ROWS, 256), bf16), wide(2 * ROWS, f32), wide(2 * ROWS, bf16)]
        + [wide(2 * ROWS, f32)]
        + [wide(ROWS, bf16)] * 10
        + [pltpu.SemaphoreType.DMA((NSEM,))] * 2
        + [pltpu.SemaphoreType.DMA((16,)), pltpu.SemaphoreType.REGULAR],
        compiler_params=pltpu.CompilerParams(
            collective_id=0, has_side_effects=True, vmem_limit_bytes=40 << 20
        ),
    )(*args)
    return pl.pallas_call(
        store,
        out_shape=shapes,
        in_specs=[pl.BlockSpec(memory_space=pl.ANY)] * 3,
        out_specs=(pl.BlockSpec(memory_space=pltpu.HBM),) * 3,
        scratch_shapes=[pltpu.SemaphoreType.DMA((3,))],
        compiler_params=pltpu.CompilerParams(vmem_limit_bytes=16 << 20),
    )(*results)


def solution(mesh):
    return jax.shard_map(
        body,
        mesh=mesh,
        in_specs=(
            P("tm", "panel", None),
            P("tm", None, "panel"),
            P("tm", "panel", None),
            P("tm", "panel", None),
            P("tm", "panel", None),
            P("tm", "panel", None),
            P("tm", "panel"),
        ),
        out_specs=(P("tm", "panel", None), P("tm", "panel", None), P("tm", "panel", None)),
        check_vma=False,
    )
```

```python
import jax
import jax.numpy as jnp
from jax import lax
from jax.experimental import pallas as pl
from jax.experimental.pallas import tpu as pltpu
from jax.sharding import PartitionSpec as P

MESH = pl.DeviceIdType.MESH
ROWS = 64
N = 1024
KEYS = (
    "a_R", "a_L", "b_Y",
    "fa_R", "fa_L", "ya_0", "ya_L", "ya_R", "b_R", "b_L", "pb_R", "pb_L",
    "fb_R", "fpb_R", "fb_L", "fpb_L", "ya_2",
    "sib_0", "sib_x", "sib_l", "sib_r", "sib_o",
)
NKEYS = len(KEYS)
SWAP0 = 4 * NKEYS
RET0 = SWAP0 + 4
NSEM = RET0 + 10
SPLIT = ((32, 16, 16),) * 4


SEQ = (('s1', 0), ('s1', 1), ('s1', 2), ('o2', 0), ('s2', 0), ('s1', 3), ('o2', 1), ('s2', 1), ('s3', 0), ('o2', 2), ('s2', 2), ('s3', 1), ('s4a', 0), ('s4b', 0), ('o2', 3), ('s2', 3), ('c0', 0), ('s3', 2), ('s4a', 1), ('s4b', 1), ('c1', 1), ('s3', 3), ('s4a', 2), ('s4b', 2), ('c2', 2))


def nt(left, right):
    return lax.dot_general(left, right, (((1,), (1,)), ((), ())), preferred_element_type=jnp.float32)


def nn(left, right):
    return jnp.dot(left, right, preferred_element_type=jnp.float32)


def kernel(
    kept_ref, cin_ref, cout_ref, w_ref, sk_ref, s_ref, obs_ref,
    block_ref, coup_ref, src_ref,
    fw, fs, fo, fi, keptv, skv, obsv, cc, xt, vacc, vb, r45,
    send13, send4, send2, send5, recv13, recv4, recv2, recv5,
    ssem, rsem, lsem, ready,
):
    kept_n = lax.axis_size("tm")
    k = lax.axis_index("tm")
    panel = lax.axis_index("panel")
    x, y = lax.rem(panel, 4), panel // 4
    core = lax.rem(k, 2)
    half = y // 2
    home = core == half
    guest = core != half
    py = jnp.where(home, y, 3 - y)
    pyq = py + 1 - 2 * lax.rem(py, 2)
    job = k - core + half
    mine = py * 4 + x

    right = {"panel": y * 4 + lax.rem(x + 1, 4)}
    left = {"panel": y * 4 + lax.rem(x + 3, 4)}
    across = {"panel": (y + 1 - 2 * lax.rem(y, 2)) * 4 + x}
    sibling = {"tm": k + 1 - 2 * core}
    partner = {"tm": k + 1 - 2 * core, "panel": (3 - y) * 4 + x}
    follower = {"tm": lax.rem(job + 1, kept_n), "panel": mine}
    has_follower = job + 1 < kept_n
    has_leader = k > 0
    before = jnp.maximum(k - 1, 0)
    before_core = lax.rem(before, 2)
    before_home = before_core == half
    leader = {
        "tm": jnp.where(before_home, before, before + 1 - 2 * before_core),
        "panel": jnp.where(before_home, panel, (3 - y) * 4 + x),
    }

    load_kept = pltpu.make_async_copy(kept_ref.at[0], keptv, lsem.at[0])
    load_sk = pltpu.make_async_copy(sk_ref.at[0], skv, lsem.at[1])
    load_obs = pltpu.make_async_copy(obs_ref, obsv, lsem.at[2])

    barrier = pltpu.get_barrier_semaphore()
    for peer in (right, left, across, sibling):
        pl.semaphore_signal(barrier, inc=1, device_id=peer, device_id_type=MESH)

    @pl.when(guest)
    def _():
        pl.semaphore_signal(barrier, inc=1, device_id=partner, device_id_type=MESH)

    @pl.when(has_follower)
    def _():
        pl.semaphore_signal(barrier, inc=1, device_id=follower, device_id_type=MESH)

    full = (fw, fs, fo, fi)
    own = (w_ref.at[0], s_ref.at[0], cout_ref.at[0], cin_ref.at[0])

    def rows(m, p, r0, n):
        return full[m].at[pl.ds(pl.multiple_of(p * ROWS + r0, 16), n)]

    def home_copy(m):
        return pltpu.make_async_copy(own[m], rows(m, panel, 0, ROWS), lsem.at[3 + m])

    def guest_copy(m):
        return pltpu.make_async_remote_copy(
            src_ref=own[m], dst_ref=rows(m, panel, 0, ROWS),
            send_sem=ssem.at[SWAP0 + m], recv_sem=rsem.at[SWAP0 + m],
            device_id=partner, device_id_type=MESH,
        )

    @pl.when(home)
    def _():
        for m in range(4):
            home_copy(m).start()

    load_kept.start()
    load_sk.start()
    load_obs.start()

    @pl.when(k == 0)
    def _():
        recv2[...] = jnp.zeros_like(recv2)
        recv5[...] = jnp.zeros_like(recv5)

    pl.semaphore_wait(barrier, 4 + guest.astype(jnp.int32) + has_leader.astype(jnp.int32))

    @pl.when(guest)
    def _():
        for m in range(4):
            guest_copy(m).start()

    @pl.when(has_leader)
    def _():
        pl.semaphore_signal(ready, inc=1, device_id=leader, device_id_type=MESH)

    def swapped(m):
        @pl.when(home)
        def _():
            home_copy(m).wait()

        @pl.when(guest)
        def _():
            guest_copy(m).wait_recv()

    copies = {}

    def send(m, key, p, r0, n, peer):
        if n == 0:
            return
        at = m * NKEYS + KEYS.index(key)
        copy = pltpu.make_async_remote_copy(
            src_ref=rows(m, p, r0, n), dst_ref=rows(m, p, r0, n),
            send_sem=ssem.at[at], recv_sem=rsem.at[at],
            device_id=peer, device_id_type=MESH,
        )
        copy.start()
        copies[m, key] = copy

    def got(m, *keys):
        for key in keys:
            if (m, key) in copies:
                copies[m, key].wait_recv()

    xl, xr, xo = lax.rem(x + 3, 4), lax.rem(x + 1, 4), lax.rem(x + 2, 4)
    row, rowq = py * 4, pyq * 4

    def s1(m):
        a = SPLIT[m][0]
        swapped(m)
        send(m, "a_R", mine, 0, a, right)
        send(m, "a_L", mine, 0, a, left)
        send(m, "b_Y", mine, a, ROWS - a, across)

    def o2(m):
        a = SPLIT[m][0]
        send(m, "ya_0", mine, 0, a, across)
        send(m, "b_R", mine, a, ROWS - a, right)
        send(m, "b_L", mine, a, ROWS - a, left)

    def s2(m):
        a, ra, _ = SPLIT[m]
        got(m, "a_R")
        send(m, "fa_R", row + xl, 0, ra, right)
        got(m, "a_L")
        send(m, "fa_L", row + xr, ra, a - ra, left)
        send(m, "ya_L", row + xl, 0, a, across)
        send(m, "ya_R", row + xr, 0, a, across)
        got(m, "b_Y")
        send(m, "pb_R", rowq + x, a, ROWS - a, right)
        send(m, "pb_L", rowq + x, a, ROWS - a, left)

    def s3(m):
        a, _, rb = SPLIT[m]
        got(m, "fa_R", "fa_L")
        send(m, "ya_2", row + xo, 0, a, across)
        got(m, "b_R")
        send(m, "fb_R", row + xl, a, rb, right)
        got(m, "b_L")
        send(m, "fb_L", row + xr, a + rb, ROWS - a - rb, left)
        got(m, "pb_R")
        send(m, "fpb_R", rowq + xl, a, rb, right)
        got(m, "pb_L")
        send(m, "fpb_L", rowq + xr, a + rb, ROWS - a - rb, left)

    def s4a(m):
        got(m, "fb_R", "fb_L")
        send(m, "sib_0", row, 0, 4 * ROWS, sibling)

    def s4b(m):
        got(m, "ya_0")
        send(m, "sib_x", rowq + x, 0, ROWS, sibling)
        got(m, "ya_L")
        send(m, "sib_l", rowq + xl, 0, ROWS, sibling)
        got(m, "ya_R")
        send(m, "sib_r", rowq + xr, 0, ROWS, sibling)
        got(m, "fpb_R", "fpb_L", "ya_2")
        send(m, "sib_o", rowq + xo, 0, ROWS, sibling)

    def s5(m):
        got(m, "sib_0", "sib_x", "sib_l", "sib_r", "sib_o")

    def back(at, src, dst, peer):
        return pltpu.make_async_remote_copy(
            src_ref=src, dst_ref=dst, send_sem=ssem.at[RET0 + at], recv_sem=rsem.at[RET0 + at],
            device_id=peer, device_id_type=MESH,
        )

    def span(p):
        return pl.ds(pl.multiple_of(p * 256, 256), 256)

    cols = [pl.ds(256 * i, 256) for i in range(4)]
    groups = [span(p) for p in (py, 3 - py, pyq, 3 - pyq)]
    theirs = [span(p) for p in (3 - py, py, 3 - pyq, pyq)]
    ret4 = back(0, send4, recv4, partner)
    ret5 = back(1, send5, recv5, follower)
    ret13 = [back(2 + i, send13.at[:, groups[i]], recv13.at[:, groups[i]], partner) for i in range(4)]
    ret2 = [back(6 + i, send2.at[:, cols[i]], recv2.at[:, cols[i]], follower) for i in range(4)]

    def c0(m):
        s5(m)
        cc[0:ROWS, :] = fi[pl.ds(pl.multiple_of(mine * ROWS, ROWS), ROWS), :]
        cc[ROWS:, :] = fo[pl.ds(pl.multiple_of(mine * ROWS, ROWS), ROWS), :]
        for i in range(4):
            part = fw[cols[i], :]
            xt[...] = nt(cc[...], part).astype(jnp.bfloat16)
            if i == 0:
                vacc[...] = nn(xt[...], part)
            else:
                vacc[...] += nn(xt[...], part)
        vb[...] = vacc[...].astype(jnp.bfloat16)

    def c1(m):
        s5(m)
        for i in range(4):
            part = nn(vb[:, cols[i]], fs[cols[i], :])
            if i == 0:
                r45[...] = part
            else:
                r45[...] += part
        send5[...] = r45[ROWS:, :].astype(jnp.bfloat16)

        @pl.when(has_follower)
        def _():
            pl.semaphore_wait(ready, 1)
            ret5.start()

        @pl.when(guest)
        def _():
            send4[...] = r45[:ROWS, :].astype(jnp.bfloat16)
            ret4.start()


    def c2(m):
        s5(m)
        for i in range(4):
            send2[:, cols[i]] = nt(vb[ROWS:, :], fo[cols[i], :]).astype(jnp.bfloat16)

            @pl.when(has_follower)
            def _():
                ret2[i].start()


    for step, m in SEQ:
        {"s1": s1, "o2": o2, "s2": s2, "s3": s3, "s4a": s4a, "s4b": s4b, "c0": c0, "c1": c1, "c2": c2}[step](m)
    def c3(i):
        both = nt(vb[...], fi[groups[i], :])

        @pl.when(home)
        def _():
            block_ref[0, :, groups[i]] = -both[:ROWS, :]
            coup_ref[0, :, groups[i]] = -both[ROWS:, :]

        @pl.when(guest)
        def _():
            send13[:, groups[i]] = both.astype(jnp.bfloat16)
            ret13[i].start()

    s4a(3)
    c3(0)
    got(3, "ya_0")
    send(3, "sib_x", rowq + x, 0, ROWS, sibling)
    got(3, "ya_L")
    send(3, "sib_l", rowq + xl, 0, ROWS, sibling)
    got(3, "ya_R")
    send(3, "sib_r", rowq + xr, 0, ROWS, sibling)
    got(3, "sib_0")
    c3(1)
    got(3, "fpb_R", "fpb_L", "ya_2")
    send(3, "sib_o", rowq + xo, 0, ROWS, sibling)
    c3(2)
    load_kept.wait()
    load_sk.wait()
    load_obs.wait()
    at = pl.ds(pl.multiple_of(panel // 2 * 128, 128), 128)
    twice = 2.0 * obsv[...].astype(jnp.float32)
    twice = jnp.concatenate([twice, twice], axis=1)
    on = lax.broadcasted_iota(jnp.int32, (ROWS, 128), 1) == (
        lax.broadcasted_iota(jnp.int32, (ROWS, 128), 0) + ROWS * lax.rem(panel, 2)
    )
    keptv[:, at] = keptv[:, at] + jnp.where(on, jnp.broadcast_to(twice, (ROWS, 128)), 0.0)

    @pl.when(has_leader)
    def _():
        ret5.wait_recv()

    @pl.when(home)
    def _():
        src_ref[0] = skv[...].astype(jnp.float32) - recv5[...].astype(jnp.float32) - r45[:ROWS, :]

    @pl.when(guest)
    def _():
        ret4.wait_recv()
        src_ref[0] = skv[...].astype(jnp.float32) - recv5[...].astype(jnp.float32) - recv4[...].astype(jnp.float32)

    got(3, "sib_x", "sib_l", "sib_r", "sib_o")
    c3(3)

    @pl.when(has_leader)
    def _():
        for i in range(4):
            ret2[i].wait_recv()

    keptv[...] = keptv[...] - recv2[...].astype(jnp.float32)

    @pl.when(home)
    def _():
        block_ref[0] = keptv[...] + block_ref[0]

    @pl.when(guest)
    def _():
        for i in range(4):
            ret13[i].wait_recv()
            block_ref[0, :, theirs[i]] = keptv[:, theirs[i]] - recv13[:ROWS, theirs[i]].astype(jnp.float32)
            coup_ref[0, :, theirs[i]] = -recv13[ROWS:, theirs[i]].astype(jnp.float32)

    for copy in copies.values():
        copy.wait_send()

    @pl.when(guest)
    def _():
        for m in range(4):
            guest_copy(m).wait_send()
        ret4.wait_send()
        for i in range(4):
            ret13[i].wait_send()

    @pl.when(has_follower)
    def _():
        ret5.wait_send()
        for i in range(4):
            ret2[i].wait_send()


def store(*refs):
    ins, outs, sem = refs[:3], refs[3:6], refs[6]
    puts = [pltpu.make_async_copy(ins[i], outs[i], sem.at[i]) for i in range(3)]
    for copy in puts:
        copy.start()
    for copy in puts:
        copy.wait()


def body(kept_block, coupling_in, *rest):
    args = (kept_block, jnp.swapaxes(coupling_in, 1, 2), *rest)
    args = tuple(pltpu.with_memory_space_constraint(a, pltpu.HBM) for a in args)
    bf16, f32 = jnp.bfloat16, jnp.float32
    vmem = pltpu.VMEM
    wide = lambda rows, dtype: vmem((rows, N), dtype)
    shapes = tuple(jax.ShapeDtypeStruct((1, ROWS, N), f32) for _ in range(3))
    results = pl.pallas_call(
        kernel,
        out_shape=shapes,
        in_specs=[pl.BlockSpec(memory_space=pltpu.HBM)] * 7,
        out_specs=(pl.BlockSpec(memory_space=pltpu.VMEM),) * 3,
        scratch_shapes=[wide(N, bf16)] * 4
        + [wide(ROWS, f32), wide(ROWS, bf16), vmem((1, ROWS), jnp.int32)]
        + [wide(2 * ROWS, bf16), vmem((2 * ROWS, 256), bf16), wide(2 * ROWS, f32), wide(2 * ROWS, bf16)]
        + [wide(2 * ROWS, f32)]
        + [wide(2 * ROWS, bf16)] + [wide(ROWS, bf16)] * 3 + [wide(2 * ROWS, bf16)] + [wide(ROWS, bf16)] * 3
        + [pltpu.SemaphoreType.DMA((NSEM,))] * 2
        + [pltpu.SemaphoreType.DMA((16,)), pltpu.SemaphoreType.REGULAR],
        compiler_params=pltpu.CompilerParams(
            collective_id=0, has_side_effects=True, vmem_limit_bytes=40 << 20
        ),
    )(*args)
    return pl.pallas_call(
        store,
        out_shape=shapes,
        in_specs=[pl.BlockSpec(memory_space=pl.ANY)] * 3,
        out_specs=(pl.BlockSpec(memory_space=pltpu.HBM),) * 3,
        scratch_shapes=[pltpu.SemaphoreType.DMA((3,))],
        compiler_params=pltpu.CompilerParams(vmem_limit_bytes=16 << 20),
    )(*results)


def solution(mesh):
    return jax.shard_map(
        body,
        mesh=mesh,
        in_specs=(
            P("tm", "panel", None),
            P("tm", None, "panel"),
            P("tm", "panel", None),
            P("tm", "panel", None),
            P("tm", "panel", None),
            P("tm", "panel", None),
            P("tm", "panel"),
        ),
        out_specs=(P("tm", "panel", None), P("tm", "panel", None), P("tm", "panel", None)),
        check_vma=False,
    )
```

```python
import jax
import jax.numpy as jnp
from jax import lax
from jax.experimental import pallas as pl
from jax.experimental.pallas import tpu as pltpu
from jax.sharding import PartitionSpec as P

MESH = pl.DeviceIdType.MESH
ROWS = 64
N = 1024
KEYS = (
    "a_R", "a_L", "b_Y",
    "fa_R", "fa_L", "ya_0", "ya_L", "ya_R", "b_R", "b_L", "pb_R", "pb_L",
    "fb_R", "fpb_R", "fb_L", "fpb_L", "ya_2",
    "sib_0", "sib_x", "sib_l", "sib_r", "sib_o",
)
NKEYS = len(KEYS)
SWAP0 = 4 * NKEYS
RET0 = SWAP0 + 4
NSEM = RET0 + 10
SPLIT = ((32, 16, 16),) * 4


SEQ = (('s1', 0), ('s1', 1), ('s1', 2), ('o2', 0), ('s2', 0), ('s1', 3), ('o2', 1), ('s2', 1), ('s3', 0), ('o2', 2), ('s2', 2), ('s3', 1), ('s4a', 0), ('s4b', 0), ('o2', 3), ('s2', 3), ('c0', 0), ('c0', 1), ('s3', 2), ('s4a', 1), ('s4b', 1), ('c1', 0), ('c1', 1), ('s3', 3), ('s4a', 2), ('s4b', 2), ('c2', 0), ('c2', 1))


def nt(left, right):
    return lax.dot_general(left, right, (((1,), (1,)), ((), ())), preferred_element_type=jnp.float32)


def nn(left, right):
    return jnp.dot(left, right, preferred_element_type=jnp.float32)


def kernel(
    kept_ref, cin_ref, cout_ref, w_ref, sk_ref, s_ref, obs_ref,
    block_ref, coup_ref, src_ref,
    fw, fs, fo, fi, keptv, skv, obsv, cc, xt, vacc, vb, r45,
    send13, send4, send2, send5, recv13, recv4, recv2, recv5,
    ssem, rsem, lsem, ready,
):
    kept_n = lax.axis_size("tm")
    k = lax.axis_index("tm")
    panel = lax.axis_index("panel")
    x, y = lax.rem(panel, 4), panel // 4
    core = lax.rem(k, 2)
    half = y // 2
    home = core == half
    guest = core != half
    py = jnp.where(home, y, 3 - y)
    pyq = py + 1 - 2 * lax.rem(py, 2)
    job = k - core + half
    mine = py * 4 + x

    right = {"panel": y * 4 + lax.rem(x + 1, 4)}
    left = {"panel": y * 4 + lax.rem(x + 3, 4)}
    across = {"panel": (y + 1 - 2 * lax.rem(y, 2)) * 4 + x}
    sibling = {"tm": k + 1 - 2 * core}
    partner = {"tm": k + 1 - 2 * core, "panel": (3 - y) * 4 + x}
    follower = {"tm": lax.rem(job + 1, kept_n), "panel": mine}
    has_follower = job + 1 < kept_n
    has_leader = k > 0
    before = jnp.maximum(k - 1, 0)
    before_core = lax.rem(before, 2)
    before_home = before_core == half
    leader = {
        "tm": jnp.where(before_home, before, before + 1 - 2 * before_core),
        "panel": jnp.where(before_home, panel, (3 - y) * 4 + x),
    }

    load_kept = pltpu.make_async_copy(kept_ref.at[0], keptv, lsem.at[0])
    load_sk = pltpu.make_async_copy(sk_ref.at[0], skv, lsem.at[1])
    load_obs = pltpu.make_async_copy(obs_ref, obsv, lsem.at[2])

    barrier = pltpu.get_barrier_semaphore()
    for peer in (right, left, across, sibling):
        pl.semaphore_signal(barrier, inc=1, device_id=peer, device_id_type=MESH)

    @pl.when(guest)
    def _():
        pl.semaphore_signal(barrier, inc=1, device_id=partner, device_id_type=MESH)

    @pl.when(has_follower)
    def _():
        pl.semaphore_signal(barrier, inc=1, device_id=follower, device_id_type=MESH)

    full = (fw, fs, fo, fi)
    own = (w_ref.at[0], s_ref.at[0], cout_ref.at[0], cin_ref.at[0])

    def rows(m, p, r0, n):
        return full[m].at[pl.ds(pl.multiple_of(p * ROWS + r0, 16), n)]

    def home_copy(m):
        return pltpu.make_async_copy(own[m], rows(m, panel, 0, ROWS), lsem.at[3 + m])

    def guest_copy(m):
        return pltpu.make_async_remote_copy(
            src_ref=own[m], dst_ref=rows(m, panel, 0, ROWS),
            send_sem=ssem.at[SWAP0 + m], recv_sem=rsem.at[SWAP0 + m],
            device_id=partner, device_id_type=MESH,
        )

    @pl.when(home)
    def _():
        for m in range(4):
            home_copy(m).start()

    load_kept.start()
    load_sk.start()
    load_obs.start()

    @pl.when(k == 0)
    def _():
        recv2[...] = jnp.zeros_like(recv2)
        recv5[...] = jnp.zeros_like(recv5)

    pl.semaphore_wait(barrier, 4 + guest.astype(jnp.int32) + has_leader.astype(jnp.int32))

    @pl.when(guest)
    def _():
        for m in range(4):
            guest_copy(m).start()

    @pl.when(has_leader)
    def _():
        pl.semaphore_signal(ready, inc=1, device_id=leader, device_id_type=MESH)

    def swapped(m):
        @pl.when(home)
        def _():
            home_copy(m).wait()

        @pl.when(guest)
        def _():
            guest_copy(m).wait_recv()

    copies = {}

    def send(m, key, p, r0, n, peer, start=True):
        if n == 0:
            return
        at = m * NKEYS + KEYS.index(key)
        copy = pltpu.make_async_remote_copy(
            src_ref=rows(m, p, r0, n), dst_ref=rows(m, p, r0, n),
            send_sem=ssem.at[at], recv_sem=rsem.at[at],
            device_id=peer, device_id_type=MESH,
        )
        if start:
            copy.start()
        copies[m, key] = copy

    def got(m, *keys):
        for key in keys:
            if (m, key) in copies:
                copies[m, key].wait_recv()

    xl, xr, xo = lax.rem(x + 3, 4), lax.rem(x + 1, 4), lax.rem(x + 2, 4)
    row, rowq = py * 4, pyq * 4

    def s1(m):
        a = SPLIT[m][0]
        swapped(m)
        send(m, "a_R", mine, 0, a, right)
        send(m, "a_L", mine, 0, a, left)
        send(m, "b_Y", mine, a, ROWS - a, across)

    def o2(m):
        a = SPLIT[m][0]
        send(m, "ya_0", mine, 0, a, across)
        send(m, "b_R", mine, a, ROWS - a, right)
        send(m, "b_L", mine, a, ROWS - a, left)

    def s2(m):
        a, ra, _ = SPLIT[m]
        got(m, "a_R")
        send(m, "fa_R", row + xl, 0, ra, right)
        got(m, "a_L")
        send(m, "fa_L", row + xr, ra, a - ra, left)
        send(m, "ya_L", row + xl, 0, a, across)
        send(m, "ya_R", row + xr, 0, a, across)
        got(m, "b_Y")
        send(m, "pb_R", rowq + x, a, ROWS - a, right)
        send(m, "pb_L", rowq + x, a, ROWS - a, left)

    def s3(m):
        a, _, rb = SPLIT[m]
        got(m, "fa_R", "fa_L")
        send(m, "ya_2", row + xo, 0, a, across)
        got(m, "b_R")
        send(m, "fb_R", row + xl, a, rb, right)
        got(m, "b_L")
        send(m, "fb_L", row + xr, a + rb, ROWS - a - rb, left)
        got(m, "pb_R")
        send(m, "fpb_R", rowq + xl, a, rb, right)
        got(m, "pb_L")
        send(m, "fpb_L", rowq + xr, a + rb, ROWS - a - rb, left)

    def s4a(m):
        got(m, "fb_R", "fb_L")
        send(m, "sib_0", row, 0, 4 * ROWS, sibling)

    def s4b(m):
        got(m, "ya_0")
        send(m, "sib_x", rowq + x, 0, ROWS, sibling)
        got(m, "ya_L")
        send(m, "sib_l", rowq + xl, 0, ROWS, sibling)
        got(m, "ya_R")
        send(m, "sib_r", rowq + xr, 0, ROWS, sibling)
        got(m, "fpb_R", "fpb_L", "ya_2")
        send(m, "sib_o", rowq + xo, 0, ROWS, sibling)

    def back(at, src, dst, peer):
        return pltpu.make_async_remote_copy(
            src_ref=src, dst_ref=dst, send_sem=ssem.at[RET0 + at], recv_sem=rsem.at[RET0 + at],
            device_id=peer, device_id_type=MESH,
        )

    def span(p):
        return pl.ds(pl.multiple_of(p * 256, 256), 256)

    spans = [span(p) for p in (py, pyq, 3 - py, 3 - pyq)]
    groups = [span(p) for p in (py, 3 - py, jnp.where(home, pyq, 3 - pyq), jnp.where(home, 3 - pyq, pyq))]
    theirs = [span(p) for p in (3 - py, py, pyq, 3 - pyq)]
    ret4 = back(0, send4, recv4, partner)
    ret5 = back(1, send5, recv5, follower)
    ret13 = [back(2 + i, send13.at[:, groups[i]], recv13.at[:, groups[i]], partner) for i in range(4)]
    ret2 = [back(6 + i, send2.at[:, spans[i]], recv2.at[:, spans[i]], follower) for i in range(4)]

    def need(m, i):
        if i == 2:
            got(m, "sib_0")
        if i == 3:
            got(m, "sib_x", "sib_l", "sib_r", "sib_o")

    def c0(half_of):
        if half_of == 0:
            cc[0:ROWS, :] = fi[pl.ds(pl.multiple_of(mine * ROWS, ROWS), ROWS), :]
            cc[ROWS:, :] = fo[pl.ds(pl.multiple_of(mine * ROWS, ROWS), ROWS), :]
        for i in (2 * half_of, 2 * half_of + 1):
            need(0, i)
            part = fw[spans[i], :]
            xt[...] = nt(cc[...], part).astype(jnp.bfloat16)
            if i == 0:
                vacc[...] = nn(xt[...], part)
            else:
                vacc[...] += nn(xt[...], part)
        if half_of == 1:
            vb[...] = vacc[...].astype(jnp.bfloat16)

    def c1(half_of):
        for i in (2 * half_of, 2 * half_of + 1):
            need(1, i)
            part = nn(vb[:, spans[i]], fs[spans[i], :])
            if i == 0:
                r45[...] = part
            else:
                r45[...] += part
        if half_of == 0:
            return
        send5[...] = r45[ROWS:, :].astype(jnp.bfloat16)

        @pl.when(has_follower)
        def _():
            pl.semaphore_wait(ready, 1)
            ret5.start()

        @pl.when(guest)
        def _():
            send4[...] = r45[:ROWS, :].astype(jnp.bfloat16)
            ret4.start()

    def c2(half_of):
        for i in (2 * half_of, 2 * half_of + 1):
            need(2, i)
            send2[:, spans[i]] = nt(vb[ROWS:, :], fo[spans[i], :]).astype(jnp.bfloat16)

            @pl.when(has_follower)
            def _():
                ret2[i].start()

    steps = {"s1": s1, "o2": o2, "s2": s2, "s3": s3, "s4a": s4a, "s4b": s4b, "c0": c0, "c1": c1, "c2": c2}
    for step, m in SEQ:
        steps[step](m)

    def stay(i):
        both = nt(vb[...], fi[groups[i], :])
        block_ref[0, :, groups[i]] = -both[:ROWS, :]
        coup_ref[0, :, groups[i]] = -both[ROWS:, :]

    def give(i):
        send13[:, groups[i]] = nt(vb[...], fi[groups[i], :]).astype(jnp.bfloat16)
        ret13[i].start()

    def c3(i):
        @pl.when(home)
        def _():
            stay(i)

        @pl.when(guest)
        def _():
            give(i)

    s4a(3)
    c3(0)
    got(3, "ya_0")
    send(3, "sib_x", rowq + x, 0, ROWS, sibling)
    got(3, "ya_L")
    send(3, "sib_l", rowq + xl, 0, ROWS, sibling)
    got(3, "ya_R")
    send(3, "sib_r", rowq + xr, 0, ROWS, sibling)
    got(3, "sib_0")
    c3(1)
    send(3, "sib_o", rowq + xo, 0, ROWS, sibling, False)
    last = ("fpb_R", "fpb_L", "ya_2")
    others = ("sib_x", "sib_l", "sib_r", "sib_o")

    @pl.when(home)
    def _():
        got(3, *last)
        copies[3, "sib_o"].start()
        stay(2)

    @pl.when(guest)
    def _():
        got(3, *others)
        give(2)
        got(3, *last)
        copies[3, "sib_o"].start()
        give(3)

    load_kept.wait()
    load_sk.wait()
    load_obs.wait()
    at = pl.ds(pl.multiple_of(panel // 2 * 128, 128), 128)
    twice = 2.0 * obsv[...].astype(jnp.float32)
    twice = jnp.concatenate([twice, twice], axis=1)
    on = lax.broadcasted_iota(jnp.int32, (ROWS, 128), 1) == (
        lax.broadcasted_iota(jnp.int32, (ROWS, 128), 0) + ROWS * lax.rem(panel, 2)
    )
    keptv[:, at] = keptv[:, at] + jnp.where(on, jnp.broadcast_to(twice, (ROWS, 128)), 0.0)

    @pl.when(has_leader)
    def _():
        ret5.wait_recv()

    @pl.when(home)
    def _():
        src_ref[0] = skv[...].astype(jnp.float32) - recv5[...].astype(jnp.float32) - r45[:ROWS, :]

    @pl.when(guest)
    def _():
        ret4.wait_recv()
        src_ref[0] = skv[...].astype(jnp.float32) - recv5[...].astype(jnp.float32) - recv4[...].astype(jnp.float32)

    @pl.when(home)
    def _():
        got(3, *others)
        stay(3)

    for copy in copies.values():
        copy.wait_send()

    @pl.when(has_leader)
    def _():
        for i in range(4):
            ret2[i].wait_recv()

    keptv[...] = keptv[...] - recv2[...].astype(jnp.float32)

    @pl.when(home)
    def _():
        block_ref[0] = keptv[...] + block_ref[0]

    @pl.when(guest)
    def _():
        for m in range(4):
            guest_copy(m).wait_send()
        ret4.wait_send()
        for i in range(4):
            ret13[i].wait_recv()
            block_ref[0, :, theirs[i]] = keptv[:, theirs[i]] - recv13[:ROWS, theirs[i]].astype(jnp.float32)
            coup_ref[0, :, theirs[i]] = -recv13[ROWS:, theirs[i]].astype(jnp.float32)
        for i in range(4):
            ret13[i].wait_send()

    @pl.when(has_follower)
    def _():
        ret5.wait_send()
        for i in range(4):
            ret2[i].wait_send()


def store(*refs):
    ins, outs, sem = refs[:3], refs[3:6], refs[6]
    puts = [pltpu.make_async_copy(ins[i], outs[i], sem.at[i]) for i in range(3)]
    for copy in puts:
        copy.start()
    for copy in puts:
        copy.wait()


def body(kept_block, coupling_in, *rest):
    args = (kept_block, jnp.swapaxes(coupling_in, 1, 2), *rest)
    args = tuple(pltpu.with_memory_space_constraint(a, pltpu.HBM) for a in args)
    bf16, f32 = jnp.bfloat16, jnp.float32
    vmem = pltpu.VMEM
    wide = lambda rows, dtype: vmem((rows, N), dtype)
    shapes = tuple(jax.ShapeDtypeStruct((1, ROWS, N), f32) for _ in range(3))
    results = pl.pallas_call(
        kernel,
        out_shape=shapes,
        in_specs=[pl.BlockSpec(memory_space=pltpu.HBM)] * 7,
        out_specs=(pl.BlockSpec(memory_space=pltpu.VMEM),) * 3,
        scratch_shapes=[wide(N, bf16)] * 4
        + [wide(ROWS, f32), wide(ROWS, bf16), vmem((1, ROWS), jnp.int32)]
        + [wide(2 * ROWS, bf16), vmem((2 * ROWS, 256), bf16), wide(2 * ROWS, f32), wide(2 * ROWS, bf16)]
        + [wide(2 * ROWS, f32)]
        + [wide(2 * ROWS, bf16)] + [wide(ROWS, bf16)] * 3 + [wide(2 * ROWS, bf16)] + [wide(ROWS, bf16)] * 3
        + [pltpu.SemaphoreType.DMA((NSEM,))] * 2
        + [pltpu.SemaphoreType.DMA((16,)), pltpu.SemaphoreType.REGULAR],
        compiler_params=pltpu.CompilerParams(
            collective_id=0, has_side_effects=True, vmem_limit_bytes=40 << 20
        ),
    )(*args)
    return pl.pallas_call(
        store,
        out_shape=shapes,
        in_specs=[pl.BlockSpec(memory_space=pl.ANY)] * 3,
        out_specs=(pl.BlockSpec(memory_space=pltpu.HBM),) * 3,
        scratch_shapes=[pltpu.SemaphoreType.DMA((3,))],
        compiler_params=pltpu.CompilerParams(vmem_limit_bytes=16 << 20),
    )(*results)


def solution(mesh):
    return jax.shard_map(
        body,
        mesh=mesh,
        in_specs=(
            P("tm", "panel", None),
            P("tm", None, "panel"),
            P("tm", "panel", None),
            P("tm", "panel", None),
            P("tm", "panel", None),
            P("tm", "panel", None),
            P("tm", "panel"),
        ),
        out_specs=(P("tm", "panel", None), P("tm", "panel", None), P("tm", "panel", None)),
        check_vma=False,
    )
```

```python
import jax
import jax.numpy as jnp
from jax import lax
from jax.experimental import pallas as pl
from jax.experimental.pallas import tpu as pltpu
from jax.sharding import PartitionSpec as P

MESH = pl.DeviceIdType.MESH
ROWS = 64
N = 1024
KEYS = (
    "a_R", "a_L", "b_Y",
    "fa_R", "fa_L", "ya_0", "ya_L", "ya_R", "b_R", "b_L", "pb_R", "pb_L",
    "fb_R", "fpb_R", "fb_L", "fpb_L", "ya_2",
    "sib_0", "sib_x", "sib_l", "sib_r", "sib_o",
)
NKEYS = len(KEYS)
SWAP0 = 4 * NKEYS
RET0 = SWAP0 + 5
NSEM = RET0 + 10
SPLIT = ((32, 16, 16), (32, 16, 16), (32, 16, 16), (16, 16, 16))


SEQ = (('s1', 0), ('s1', 1), ('s1', 2), ('o2', 0), ('s2', 0), ('s1', 3), ('o2', 1), ('s2', 1), ('s3', 0), ('o2', 2), ('s2', 2), ('s3', 1), ('s4a', 0), ('s4b', 0), ('o2', 3), ('s2', 3), ('c0', 0), ('c0', 1), ('s3', 2), ('s4a', 1), ('s4b', 1), ('c1', 0), ('c1', 1), ('s3', 3), ('s4a', 2), ('s4b', 2), ('c2', 0), ('c2', 1))


def nt(left, right):
    return lax.dot_general(left, right, (((1,), (1,)), ((), ())), preferred_element_type=jnp.float32)


def nn(left, right):
    return jnp.dot(left, right, preferred_element_type=jnp.float32)


def kernel(
    kept_ref, cin_ref, cout_ref, w_ref, sk_ref, s_ref, obs_ref,
    block_ref, coup_ref, src_ref,
    fw, fs, fo, fi, keptv, skv, obsv, cc, xt, vacc, vb, r45,
    send13, send4, send2, send5, recv13, recv4, recv2, recv5,
    ssem, rsem, lsem, ready,
):
    kept_n = lax.axis_size("tm")
    k = lax.axis_index("tm")
    panel = lax.axis_index("panel")
    x, y = lax.rem(panel, 4), panel // 4
    core = lax.rem(k, 2)
    half = y // 2
    home = core == half
    guest = core != half
    py = jnp.where(home, y, 3 - y)
    pyq = py + 1 - 2 * lax.rem(py, 2)
    job = k - core + half
    mine = py * 4 + x

    right = {"panel": y * 4 + lax.rem(x + 1, 4)}
    left = {"panel": y * 4 + lax.rem(x + 3, 4)}
    across = {"panel": (y + 1 - 2 * lax.rem(y, 2)) * 4 + x}
    sibling = {"tm": k + 1 - 2 * core}
    partner = {"tm": k + 1 - 2 * core, "panel": (3 - y) * 4 + x}
    follower = {"tm": lax.rem(job + 1, kept_n), "panel": mine}
    has_follower = job + 1 < kept_n
    has_leader = k > 0
    before = jnp.maximum(k - 1, 0)
    before_core = lax.rem(before, 2)
    before_home = before_core == half
    leader = {
        "tm": jnp.where(before_home, before, before + 1 - 2 * before_core),
        "panel": jnp.where(before_home, panel, (3 - y) * 4 + x),
    }

    load_kept = pltpu.make_async_copy(kept_ref.at[0], keptv, lsem.at[0])
    load_sk = pltpu.make_async_copy(sk_ref.at[0], skv, lsem.at[1])
    load_obs = pltpu.make_async_copy(obs_ref, obsv, lsem.at[2])

    barrier = pltpu.get_barrier_semaphore()
    for peer in (right, left, across, sibling):
        pl.semaphore_signal(barrier, inc=1, device_id=peer, device_id_type=MESH)

    @pl.when(guest)
    def _():
        pl.semaphore_signal(barrier, inc=1, device_id=partner, device_id_type=MESH)

    @pl.when(has_follower)
    def _():
        pl.semaphore_signal(barrier, inc=1, device_id=follower, device_id_type=MESH)

    full = (fw, fs, fo, fi)
    own = (w_ref.at[0], s_ref.at[0], cout_ref.at[0], cin_ref.at[0])

    def rows(m, p, r0, n):
        return full[m].at[pl.ds(pl.multiple_of(p * ROWS + r0, 16), n)]

    def home_copy(m):
        return pltpu.make_async_copy(own[m], rows(m, panel, 0, ROWS), lsem.at[3 + m])

    def guest_copies(m):
        a = SPLIT[0][0] if m == 0 else ROWS
        pieces = ((0, a, SWAP0 + m), (a, ROWS - a, SWAP0 + 4))
        return [
            pltpu.make_async_remote_copy(
                src_ref=own[m].at[pl.ds(r0, n)], dst_ref=rows(m, panel, r0, n),
                send_sem=ssem.at[at], recv_sem=rsem.at[at],
                device_id=partner, device_id_type=MESH,
            )
            for r0, n, at in pieces
            if n
        ]

    @pl.when(home)
    def _():
        for m in range(4):
            home_copy(m).start()

    load_kept.start()
    load_sk.start()
    load_obs.start()

    @pl.when(k == 0)
    def _():
        recv2[...] = jnp.zeros_like(recv2)
        recv5[...] = jnp.zeros_like(recv5)

    pl.semaphore_wait(barrier, 4 + guest.astype(jnp.int32) + has_leader.astype(jnp.int32))

    @pl.when(guest)
    def _():
        for m in range(4):
            for copy in guest_copies(m):
                copy.start()

    @pl.when(has_leader)
    def _():
        pl.semaphore_signal(ready, inc=1, device_id=leader, device_id_type=MESH)

    def swapped(m, i=0):
        if i == 0:

            @pl.when(home)
            def _():
                home_copy(m).wait()

        if i < len(guest_copies(m)):

            @pl.when(guest)
            def _():
                guest_copies(m)[i].wait_recv()

    copies = {}

    def send(m, key, p, r0, n, peer, start=True):
        if n == 0:
            return
        at = m * NKEYS + KEYS.index(key)
        copy = pltpu.make_async_remote_copy(
            src_ref=rows(m, p, r0, n), dst_ref=rows(m, p, r0, n),
            send_sem=ssem.at[at], recv_sem=rsem.at[at],
            device_id=peer, device_id_type=MESH,
        )
        if start:
            copy.start()
        copies[m, key] = copy

    def got(m, *keys):
        for key in keys:
            if (m, key) in copies:
                copies[m, key].wait_recv()

    xl, xr, xo = lax.rem(x + 3, 4), lax.rem(x + 1, 4), lax.rem(x + 2, 4)
    row, rowq = py * 4, pyq * 4

    def s1(m):
        a = SPLIT[m][0]
        swapped(m)
        send(m, "a_R", mine, 0, a, right)
        send(m, "a_L", mine, 0, a, left)
        swapped(m, 1)
        send(m, "b_Y", mine, a, ROWS - a, across)

    def o2(m):
        a = SPLIT[m][0]
        send(m, "ya_0", mine, 0, a, across)
        send(m, "b_R", mine, a, ROWS - a, right)
        send(m, "b_L", mine, a, ROWS - a, left)

    def s2(m):
        a, ra, _ = SPLIT[m]
        got(m, "a_R")
        send(m, "fa_R", row + xl, 0, ra, right)
        got(m, "a_L")
        send(m, "fa_L", row + xr, ra, a - ra, left)
        send(m, "ya_L", row + xl, 0, a, across)
        send(m, "ya_R", row + xr, 0, a, across)
        got(m, "b_Y")
        send(m, "pb_R", rowq + x, a, ROWS - a, right)
        send(m, "pb_L", rowq + x, a, ROWS - a, left)

    def s3(m):
        a, _, rb = SPLIT[m]
        got(m, "fa_R", "fa_L")
        send(m, "ya_2", row + xo, 0, a, across)
        got(m, "b_R")
        send(m, "fb_R", row + xl, a, rb, right)
        got(m, "b_L")
        send(m, "fb_L", row + xr, a + rb, ROWS - a - rb, left)
        got(m, "pb_R")
        send(m, "fpb_R", rowq + xl, a, rb, right)
        got(m, "pb_L")
        send(m, "fpb_L", rowq + xr, a + rb, ROWS - a - rb, left)

    def s4a(m):
        got(m, "fb_R", "fb_L")
        send(m, "sib_0", row, 0, 4 * ROWS, sibling)

    def s4b(m):
        got(m, "ya_0")
        send(m, "sib_x", rowq + x, 0, ROWS, sibling)
        got(m, "ya_L")
        send(m, "sib_l", rowq + xl, 0, ROWS, sibling)
        got(m, "ya_R")
        send(m, "sib_r", rowq + xr, 0, ROWS, sibling)
        got(m, "fpb_R", "fpb_L", "ya_2")
        send(m, "sib_o", rowq + xo, 0, ROWS, sibling)

    def back(at, src, dst, peer):
        return pltpu.make_async_remote_copy(
            src_ref=src, dst_ref=dst, send_sem=ssem.at[RET0 + at], recv_sem=rsem.at[RET0 + at],
            device_id=peer, device_id_type=MESH,
        )

    def span(p):
        return pl.ds(pl.multiple_of(p * 256, 256), 256)

    spans = [span(p) for p in (py, pyq, 3 - py, 3 - pyq)]
    groups = [span(p) for p in (py, 3 - py, jnp.where(home, pyq, 3 - pyq), jnp.where(home, 3 - pyq, pyq))]
    theirs = [span(p) for p in (3 - py, py, pyq, 3 - pyq)]
    ret4 = back(0, send4, recv4, partner)
    ret5 = back(1, send5, recv5, follower)
    ret13 = [back(2 + i, send13.at[:, groups[i]], recv13.at[:, groups[i]], partner) for i in range(4)]
    ret2 = [back(6 + i, send2.at[:, spans[i]], recv2.at[:, spans[i]], follower) for i in range(4)]

    def need(m, i):
        if i == 2:
            got(m, "sib_0")
        if i == 3:
            got(m, "sib_x", "sib_l", "sib_r", "sib_o")

    def c0(half_of):
        if half_of == 0:
            cc[0:ROWS, :] = fi[pl.ds(pl.multiple_of(mine * ROWS, ROWS), ROWS), :]
            cc[ROWS:, :] = fo[pl.ds(pl.multiple_of(mine * ROWS, ROWS), ROWS), :]
        for i in (2 * half_of, 2 * half_of + 1):
            need(0, i)
            part = fw[spans[i], :]
            xt[...] = nt(cc[...], part).astype(jnp.bfloat16)
            if i == 0:
                vacc[...] = nn(xt[...], part)
            else:
                vacc[...] += nn(xt[...], part)
        if half_of == 1:
            vb[...] = vacc[...].astype(jnp.bfloat16)

    def c1(half_of):
        for i in (2 * half_of, 2 * half_of + 1):
            need(1, i)
            part = nn(vb[:, spans[i]], fs[spans[i], :])
            if i == 0:
                r45[...] = part
            else:
                r45[...] += part
        if half_of == 0:
            return
        send5[...] = r45[ROWS:, :].astype(jnp.bfloat16)

        @pl.when(has_follower)
        def _():
            pl.semaphore_wait(ready, 1)
            ret5.start()

        @pl.when(guest)
        def _():
            send4[...] = r45[:ROWS, :].astype(jnp.bfloat16)
            ret4.start()

    def c2(half_of):
        for i in (2 * half_of, 2 * half_of + 1):
            need(2, i)
            send2[:, spans[i]] = nt(vb[ROWS:, :], fo[spans[i], :]).astype(jnp.bfloat16)

            @pl.when(has_follower)
            def _():
                ret2[i].start()

    steps = {"s1": s1, "o2": o2, "s2": s2, "s3": s3, "s4a": s4a, "s4b": s4b, "c0": c0, "c1": c1, "c2": c2}
    for step, m in SEQ:
        steps[step](m)

    def stay(i):
        both = nt(vb[...], fi[groups[i], :])
        block_ref[0, :, groups[i]] = -both[:ROWS, :]
        coup_ref[0, :, groups[i]] = -both[ROWS:, :]

    def give(i):
        send13[:, groups[i]] = nt(vb[...], fi[groups[i], :]).astype(jnp.bfloat16)
        ret13[i].start()

    def c3(i):
        @pl.when(home)
        def _():
            stay(i)

        @pl.when(guest)
        def _():
            give(i)

    s4a(3)
    c3(0)
    got(3, "ya_0")
    send(3, "sib_x", rowq + x, 0, ROWS, sibling)
    got(3, "ya_L")
    send(3, "sib_l", rowq + xl, 0, ROWS, sibling)
    got(3, "ya_R")
    send(3, "sib_r", rowq + xr, 0, ROWS, sibling)
    got(3, "sib_0")
    c3(1)
    send(3, "sib_o", rowq + xo, 0, ROWS, sibling, False)
    last = ("fpb_R", "fpb_L", "ya_2")
    others = ("sib_x", "sib_l", "sib_r", "sib_o")

    @pl.when(home)
    def _():
        got(3, *last)
        copies[3, "sib_o"].start()
        stay(2)

    @pl.when(guest)
    def _():
        got(3, *others)
        give(2)
        got(3, *last)
        copies[3, "sib_o"].start()
        give(3)

    load_kept.wait()
    load_sk.wait()
    load_obs.wait()
    at = pl.ds(pl.multiple_of(panel // 2 * 128, 128), 128)
    twice = 2.0 * obsv[...].astype(jnp.float32)
    twice = jnp.concatenate([twice, twice], axis=1)
    on = lax.broadcasted_iota(jnp.int32, (ROWS, 128), 1) == (
        lax.broadcasted_iota(jnp.int32, (ROWS, 128), 0) + ROWS * lax.rem(panel, 2)
    )
    keptv[:, at] = keptv[:, at] + jnp.where(on, jnp.broadcast_to(twice, (ROWS, 128)), 0.0)

    @pl.when(has_leader)
    def _():
        ret5.wait_recv()

    @pl.when(home)
    def _():
        src_ref[0] = skv[...].astype(jnp.float32) - recv5[...].astype(jnp.float32) - r45[:ROWS, :]

    @pl.when(guest)
    def _():
        ret4.wait_recv()
        src_ref[0] = skv[...].astype(jnp.float32) - recv5[...].astype(jnp.float32) - recv4[...].astype(jnp.float32)

    @pl.when(home)
    def _():
        got(3, *others)
        stay(3)

    for copy in copies.values():
        copy.wait_send()

    @pl.when(has_leader)
    def _():
        for i in range(4):
            ret2[i].wait_recv()

    keptv[...] = keptv[...] - recv2[...].astype(jnp.float32)

    @pl.when(home)
    def _():
        block_ref[0] = keptv[...] + block_ref[0]

    @pl.when(guest)
    def _():
        for m in range(4):
            for copy in guest_copies(m):
                copy.wait_send()
        ret4.wait_send()
        for i in range(4):
            ret13[i].wait_recv()
            block_ref[0, :, theirs[i]] = keptv[:, theirs[i]] - recv13[:ROWS, theirs[i]].astype(jnp.float32)
            coup_ref[0, :, theirs[i]] = -recv13[ROWS:, theirs[i]].astype(jnp.float32)
        for i in range(4):
            ret13[i].wait_send()

    @pl.when(has_follower)
    def _():
        ret5.wait_send()
        for i in range(4):
            ret2[i].wait_send()


def store(*refs):
    ins, outs, sem = refs[:3], refs[3:6], refs[6]
    puts = [pltpu.make_async_copy(ins[i], outs[i], sem.at[i]) for i in range(3)]
    for copy in puts:
        copy.start()
    for copy in puts:
        copy.wait()


def body(kept_block, coupling_in, *rest):
    args = (kept_block, jnp.swapaxes(coupling_in, 1, 2), *rest)
    args = tuple(pltpu.with_memory_space_constraint(a, pltpu.HBM) for a in args)
    bf16, f32 = jnp.bfloat16, jnp.float32
    vmem = pltpu.VMEM
    wide = lambda rows, dtype: vmem((rows, N), dtype)
    shapes = tuple(jax.ShapeDtypeStruct((1, ROWS, N), f32) for _ in range(3))
    results = pl.pallas_call(
        kernel,
        out_shape=shapes,
        in_specs=[pl.BlockSpec(memory_space=pltpu.HBM)] * 7,
        out_specs=(pl.BlockSpec(memory_space=pltpu.VMEM),) * 3,
        scratch_shapes=[wide(N, bf16)] * 4
        + [wide(ROWS, f32), wide(ROWS, bf16), vmem((1, ROWS), jnp.int32)]
        + [wide(2 * ROWS, bf16), vmem((2 * ROWS, 256), bf16), wide(2 * ROWS, f32), wide(2 * ROWS, bf16)]
        + [wide(2 * ROWS, f32)]
        + [wide(2 * ROWS, bf16)] + [wide(ROWS, bf16)] * 3 + [wide(2 * ROWS, bf16)] + [wide(ROWS, bf16)] * 3
        + [pltpu.SemaphoreType.DMA((NSEM,))] * 2
        + [pltpu.SemaphoreType.DMA((16,)), pltpu.SemaphoreType.REGULAR],
        compiler_params=pltpu.CompilerParams(
            collective_id=0, has_side_effects=True, vmem_limit_bytes=40 << 20
        ),
    )(*args)
    return pl.pallas_call(
        store,
        out_shape=shapes,
        in_specs=[pl.BlockSpec(memory_space=pl.ANY)] * 3,
        out_specs=(pl.BlockSpec(memory_space=pltpu.HBM),) * 3,
        scratch_shapes=[pltpu.SemaphoreType.DMA((3,))],
        compiler_params=pltpu.CompilerParams(vmem_limit_bytes=16 << 20),
    )(*results)


def solution(mesh):
    return jax.shard_map(
        body,
        mesh=mesh,
        in_specs=(
            P("tm", "panel", None),
            P("tm", None, "panel"),
            P("tm", "panel", None),
            P("tm", "panel", None),
            P("tm", "panel", None),
            P("tm", "panel", None),
            P("tm", "panel"),
        ),
        out_specs=(P("tm", "panel", None), P("tm", "panel", None), P("tm", "panel", None)),
        check_vma=False,
    )
```

```python
import jax
import jax.numpy as jnp
from jax import lax
from jax.experimental import pallas as pl
from jax.experimental.pallas import tpu as pltpu
from jax.sharding import PartitionSpec as P

MESH = pl.DeviceIdType.MESH
ROWS = 64
N = 1024
KEYS = (
    "a_R", "a_L", "b_Y",
    "fa_R", "fa_L", "ya_0", "ya_L", "ya_R", "b_R", "b_L", "pb_R", "pb_L",
    "fb_R", "fpb_R", "fb_L", "fpb_L", "ya_2",
    "sib_0", "sib_x", "sib_l", "sib_r", "sib_o",
)
NKEYS = len(KEYS)
SWAP0 = 4 * NKEYS
RET0 = SWAP0 + 5
NSEM = RET0 + 10
SPLIT = ((32, 16, 16), (32, 16, 16), (32, 16, 16), (16, 16, 16))


SEQ = (('s1', 0), ('s1', 1), ('s1', 2), ('o2', 0), ('s2', 0), ('s1', 3), ('o2', 1), ('s2', 1), ('s3', 0), ('o2', 2), ('s2', 2), ('s3', 1), ('o2', 3), ('s2', 3), ('s4a', 0), ('s4b', 0), ('c0', 0), ('c0', 1), ('s3', 2), ('s4a', 1), ('s4b', 1), ('c1', 0), ('c1', 1), ('s3', 3), ('s4a', 2), ('s4b', 2), ('c2', 0), ('c2', 1))


def nt(left, right):
    return lax.dot_general(left, right, (((1,), (1,)), ((), ())), preferred_element_type=jnp.float32)


def nn(left, right):
    return jnp.dot(left, right, preferred_element_type=jnp.float32)


def kernel(
    kept_ref, cin_ref, cout_ref, w_ref, sk_ref, s_ref, obs_ref,
    block_ref, coup_ref, src_ref,
    fw, fs, fo, fi, keptv, skv, obsv, cc, xt, vacc, vb, r45,
    send13, send4, send2, send5, recv13, recv4, recv2, recv5,
    ssem, rsem, lsem, ready,
):
    kept_n = lax.axis_size("tm")
    k = lax.axis_index("tm")
    panel = lax.axis_index("panel")
    x, y = lax.rem(panel, 4), panel // 4
    core = lax.rem(k, 2)
    half = y // 2
    home = core == half
    guest = core != half
    py = jnp.where(home, y, 3 - y)
    pyq = py + 1 - 2 * lax.rem(py, 2)
    job = k - core + half
    mine = py * 4 + x

    right = {"panel": y * 4 + lax.rem(x + 1, 4)}
    left = {"panel": y * 4 + lax.rem(x + 3, 4)}
    across = {"panel": (y + 1 - 2 * lax.rem(y, 2)) * 4 + x}
    sibling = {"tm": k + 1 - 2 * core}
    partner = {"tm": k + 1 - 2 * core, "panel": (3 - y) * 4 + x}
    follower = {"tm": lax.rem(job + 1, kept_n), "panel": mine}
    has_follower = job + 1 < kept_n
    has_leader = k > 0
    before = jnp.maximum(k - 1, 0)
    before_core = lax.rem(before, 2)
    before_home = before_core == half
    leader = {
        "tm": jnp.where(before_home, before, before + 1 - 2 * before_core),
        "panel": jnp.where(before_home, panel, (3 - y) * 4 + x),
    }

    load_kept = pltpu.make_async_copy(kept_ref.at[0], keptv, lsem.at[0])
    load_sk = pltpu.make_async_copy(sk_ref.at[0], skv, lsem.at[1])
    load_obs = pltpu.make_async_copy(obs_ref, obsv, lsem.at[2])

    barrier = pltpu.get_barrier_semaphore()
    for peer in (right, left, across, sibling):
        pl.semaphore_signal(barrier, inc=1, device_id=peer, device_id_type=MESH)

    @pl.when(guest)
    def _():
        pl.semaphore_signal(barrier, inc=1, device_id=partner, device_id_type=MESH)

    @pl.when(has_follower)
    def _():
        pl.semaphore_signal(barrier, inc=1, device_id=follower, device_id_type=MESH)

    full = (fw, fs, fo, fi)
    own = (w_ref.at[0], s_ref.at[0], cout_ref.at[0], cin_ref.at[0])

    def rows(m, p, r0, n):
        return full[m].at[pl.ds(pl.multiple_of(p * ROWS + r0, 16), n)]

    def home_copy(m):
        return pltpu.make_async_copy(own[m], rows(m, panel, 0, ROWS), lsem.at[3 + m])

    def guest_copies(m):
        a = SPLIT[0][0] if m == 0 else ROWS
        pieces = ((0, a, SWAP0 + m), (a, ROWS - a, SWAP0 + 4))
        return [
            pltpu.make_async_remote_copy(
                src_ref=own[m].at[pl.ds(r0, n)], dst_ref=rows(m, panel, r0, n),
                send_sem=ssem.at[at], recv_sem=rsem.at[at],
                device_id=partner, device_id_type=MESH,
            )
            for r0, n, at in pieces
            if n
        ]

    @pl.when(home)
    def _():
        for m in range(4):
            home_copy(m).start()

    load_kept.start()
    load_sk.start()
    load_obs.start()

    @pl.when(k == 0)
    def _():
        recv2[...] = jnp.zeros_like(recv2)
        recv5[...] = jnp.zeros_like(recv5)

    pl.semaphore_wait(barrier, 4 + guest.astype(jnp.int32) + has_leader.astype(jnp.int32))

    @pl.when(guest)
    def _():
        for m in range(4):
            for copy in guest_copies(m):
                copy.start()

    @pl.when(has_leader)
    def _():
        pl.semaphore_signal(ready, inc=1, device_id=leader, device_id_type=MESH)

    def swapped(m, i=0):
        if i == 0:

            @pl.when(home)
            def _():
                home_copy(m).wait()

        if i < len(guest_copies(m)):

            @pl.when(guest)
            def _():
                guest_copies(m)[i].wait_recv()

    copies = {}

    def send(m, key, p, r0, n, peer, start=True):
        if n == 0:
            return
        at = m * NKEYS + KEYS.index(key)
        copy = pltpu.make_async_remote_copy(
            src_ref=rows(m, p, r0, n), dst_ref=rows(m, p, r0, n),
            send_sem=ssem.at[at], recv_sem=rsem.at[at],
            device_id=peer, device_id_type=MESH,
        )
        if start:
            copy.start()
        copies[m, key] = copy

    def got(m, *keys):
        for key in keys:
            if (m, key) in copies:
                copies[m, key].wait_recv()

    xl, xr, xo = lax.rem(x + 3, 4), lax.rem(x + 1, 4), lax.rem(x + 2, 4)
    row, rowq = py * 4, pyq * 4

    def s1(m):
        a = SPLIT[m][0]
        swapped(m)
        send(m, "a_R", mine, 0, a, right)
        send(m, "a_L", mine, 0, a, left)
        swapped(m, 1)
        send(m, "b_Y", mine, a, ROWS - a, across)

    def o2(m):
        a = SPLIT[m][0]
        send(m, "ya_0", mine, 0, a, across)
        send(m, "b_R", mine, a, ROWS - a, right)
        send(m, "b_L", mine, a, ROWS - a, left)

    def s2(m):
        a, ra, _ = SPLIT[m]
        got(m, "a_R")
        send(m, "fa_R", row + xl, 0, ra, right)
        got(m, "a_L")
        send(m, "fa_L", row + xr, ra, a - ra, left)
        send(m, "ya_L", row + xl, 0, a, across)
        send(m, "ya_R", row + xr, 0, a, across)
        got(m, "b_Y")
        send(m, "pb_R", rowq + x, a, ROWS - a, right)
        send(m, "pb_L", rowq + x, a, ROWS - a, left)

    def s3(m):
        a, _, rb = SPLIT[m]
        got(m, "fa_R", "fa_L")
        send(m, "ya_2", row + xo, 0, a, across)
        got(m, "b_R")
        send(m, "fb_R", row + xl, a, rb, right)
        got(m, "b_L")
        send(m, "fb_L", row + xr, a + rb, ROWS - a - rb, left)
        got(m, "pb_R")
        send(m, "fpb_R", rowq + xl, a, rb, right)
        got(m, "pb_L")
        send(m, "fpb_L", rowq + xr, a + rb, ROWS - a - rb, left)

    def s4a(m):
        got(m, "fb_R", "fb_L")
        send(m, "sib_0", row, 0, 4 * ROWS, sibling)

    def s4b(m):
        got(m, "ya_0")
        send(m, "sib_x", rowq + x, 0, ROWS, sibling)
        got(m, "ya_L")
        send(m, "sib_l", rowq + xl, 0, ROWS, sibling)
        got(m, "ya_R")
        send(m, "sib_r", rowq + xr, 0, ROWS, sibling)
        got(m, "fpb_R", "fpb_L", "ya_2")
        send(m, "sib_o", rowq + xo, 0, ROWS, sibling)

    def back(at, src, dst, peer):
        return pltpu.make_async_remote_copy(
            src_ref=src, dst_ref=dst, send_sem=ssem.at[RET0 + at], recv_sem=rsem.at[RET0 + at],
            device_id=peer, device_id_type=MESH,
        )

    def span(p):
        return pl.ds(pl.multiple_of(p * 256, 256), 256)

    spans = [span(p) for p in (py, pyq, 3 - py, 3 - pyq)]
    groups = [span(p) for p in (py, 3 - py, jnp.where(home, pyq, 3 - pyq), jnp.where(home, 3 - pyq, pyq))]
    theirs = [span(p) for p in (3 - py, py, pyq, 3 - pyq)]
    ret4 = back(0, send4, recv4, partner)
    ret5 = back(1, send5, recv5, follower)
    ret13 = [back(2 + i, send13.at[:, groups[i]], recv13.at[:, groups[i]], partner) for i in range(4)]
    ret2 = [back(6 + i, send2.at[:, spans[i]], recv2.at[:, spans[i]], follower) for i in range(4)]

    def need(m, i):
        if i == 2:
            got(m, "sib_0")
        if i == 3:
            got(m, "sib_x", "sib_l", "sib_r", "sib_o")

    def c0(half_of):
        if half_of == 0:
            cc[0:ROWS, :] = fi[pl.ds(pl.multiple_of(mine * ROWS, ROWS), ROWS), :]
            cc[ROWS:, :] = fo[pl.ds(pl.multiple_of(mine * ROWS, ROWS), ROWS), :]
        for i in (2 * half_of, 2 * half_of + 1):
            need(0, i)
            part = fw[spans[i], :]
            xt[...] = nt(cc[...], part).astype(jnp.bfloat16)
            if i == 0:
                vacc[...] = nn(xt[...], part)
            else:
                vacc[...] += nn(xt[...], part)
        if half_of == 1:
            vb[...] = vacc[...].astype(jnp.bfloat16)

    def c1(half_of):
        for i in (2 * half_of, 2 * half_of + 1):
            need(1, i)
            part = nn(vb[:, spans[i]], fs[spans[i], :])
            if i == 0:
                r45[...] = part
            else:
                r45[...] += part
        if half_of == 0:
            return
        send5[...] = r45[ROWS:, :].astype(jnp.bfloat16)

        @pl.when(has_follower)
        def _():
            pl.semaphore_wait(ready, 1)
            ret5.start()

        @pl.when(guest)
        def _():
            send4[...] = r45[:ROWS, :].astype(jnp.bfloat16)
            ret4.start()

    def c2(half_of):
        for i in (2 * half_of, 2 * half_of + 1):
            need(2, i)
            send2[:, spans[i]] = nt(vb[ROWS:, :], fo[spans[i], :]).astype(jnp.bfloat16)

            @pl.when(has_follower)
            def _():
                ret2[i].start()

    steps = {"s1": s1, "o2": o2, "s2": s2, "s3": s3, "s4a": s4a, "s4b": s4b, "c0": c0, "c1": c1, "c2": c2}
    for step, m in SEQ:
        steps[step](m)

    def stay(i):
        both = nt(vb[...], fi[groups[i], :])
        block_ref[0, :, groups[i]] = -both[:ROWS, :]
        coup_ref[0, :, groups[i]] = -both[ROWS:, :]

    def give(i):
        send13[:, groups[i]] = nt(vb[...], fi[groups[i], :]).astype(jnp.bfloat16)
        ret13[i].start()

    def c3(i):
        @pl.when(home)
        def _():
            stay(i)

        @pl.when(guest)
        def _():
            give(i)

    s4a(3)
    c3(0)
    got(3, "ya_0")
    send(3, "sib_x", rowq + x, 0, ROWS, sibling)
    got(3, "ya_L")
    send(3, "sib_l", rowq + xl, 0, ROWS, sibling)
    got(3, "ya_R")
    send(3, "sib_r", rowq + xr, 0, ROWS, sibling)
    got(3, "sib_0")
    c3(1)
    send(3, "sib_o", rowq + xo, 0, ROWS, sibling, False)
    last = ("fpb_R", "fpb_L", "ya_2")
    others = ("sib_x", "sib_l", "sib_r", "sib_o")

    @pl.when(home)
    def _():
        got(3, *last)
        copies[3, "sib_o"].start()
        stay(2)

    @pl.when(guest)
    def _():
        got(3, *others)
        give(2)
        got(3, *last)
        copies[3, "sib_o"].start()
        give(3)

    load_kept.wait()
    load_sk.wait()
    load_obs.wait()
    at = pl.ds(pl.multiple_of(panel // 2 * 128, 128), 128)
    twice = 2.0 * obsv[...].astype(jnp.float32)
    twice = jnp.concatenate([twice, twice], axis=1)
    on = lax.broadcasted_iota(jnp.int32, (ROWS, 128), 1) == (
        lax.broadcasted_iota(jnp.int32, (ROWS, 128), 0) + ROWS * lax.rem(panel, 2)
    )
    keptv[:, at] = keptv[:, at] + jnp.where(on, jnp.broadcast_to(twice, (ROWS, 128)), 0.0)

    @pl.when(has_leader)
    def _():
        ret5.wait_recv()

    @pl.when(home)
    def _():
        src_ref[0] = skv[...].astype(jnp.float32) - recv5[...].astype(jnp.float32) - r45[:ROWS, :]

    @pl.when(guest)
    def _():
        ret4.wait_recv()
        src_ref[0] = skv[...].astype(jnp.float32) - recv5[...].astype(jnp.float32) - recv4[...].astype(jnp.float32)

    @pl.when(home)
    def _():
        got(3, *others)
        stay(3)

    for copy in copies.values():
        copy.wait_send()

    @pl.when(has_leader)
    def _():
        for i in range(4):
            ret2[i].wait_recv()

    keptv[...] = keptv[...] - recv2[...].astype(jnp.float32)

    @pl.when(home)
    def _():
        block_ref[0] = keptv[...] + block_ref[0]

    @pl.when(guest)
    def _():
        for m in range(4):
            for copy in guest_copies(m):
                copy.wait_send()
        ret4.wait_send()
        for i in range(4):
            ret13[i].wait_recv()
            block_ref[0, :, theirs[i]] = keptv[:, theirs[i]] - recv13[:ROWS, theirs[i]].astype(jnp.float32)
            coup_ref[0, :, theirs[i]] = -recv13[ROWS:, theirs[i]].astype(jnp.float32)
        for i in range(4):
            ret13[i].wait_send()

    @pl.when(has_follower)
    def _():
        ret5.wait_send()
        for i in range(4):
            ret2[i].wait_send()


def store(*refs):
    ins, outs, sem = refs[:3], refs[3:6], refs[6]
    puts = [pltpu.make_async_copy(ins[i], outs[i], sem.at[i]) for i in range(3)]
    for copy in puts:
        copy.start()
    for copy in puts:
        copy.wait()


def body(kept_block, coupling_in, *rest):
    args = (kept_block, jnp.swapaxes(coupling_in, 1, 2), *rest)
    args = tuple(pltpu.with_memory_space_constraint(a, pltpu.HBM) for a in args)
    bf16, f32 = jnp.bfloat16, jnp.float32
    vmem = pltpu.VMEM
    wide = lambda rows, dtype: vmem((rows, N), dtype)
    shapes = tuple(jax.ShapeDtypeStruct((1, ROWS, N), f32) for _ in range(3))
    results = pl.pallas_call(
        kernel,
        out_shape=shapes,
        in_specs=[pl.BlockSpec(memory_space=pltpu.HBM)] * 7,
        out_specs=(pl.BlockSpec(memory_space=pltpu.VMEM),) * 3,
        scratch_shapes=[wide(N, bf16)] * 4
        + [wide(ROWS, f32), wide(ROWS, bf16), vmem((1, ROWS), jnp.int32)]
        + [wide(2 * ROWS, bf16), vmem((2 * ROWS, 256), bf16), wide(2 * ROWS, f32), wide(2 * ROWS, bf16)]
        + [wide(2 * ROWS, f32)]
        + [wide(2 * ROWS, bf16)] + [wide(ROWS, bf16)] * 3 + [wide(2 * ROWS, bf16)] + [wide(ROWS, bf16)] * 3
        + [pltpu.SemaphoreType.DMA((NSEM,))] * 2
        + [pltpu.SemaphoreType.DMA((16,)), pltpu.SemaphoreType.REGULAR],
        compiler_params=pltpu.CompilerParams(
            collective_id=0, has_side_effects=True, vmem_limit_bytes=40 << 20
        ),
    )(*args)
    return pl.pallas_call(
        store,
        out_shape=shapes,
        in_specs=[pl.BlockSpec(memory_space=pl.ANY)] * 3,
        out_specs=(pl.BlockSpec(memory_space=pltpu.HBM),) * 3,
        scratch_shapes=[pltpu.SemaphoreType.DMA((3,))],
        compiler_params=pltpu.CompilerParams(vmem_limit_bytes=16 << 20),
    )(*results)


def solution(mesh):
    return jax.shard_map(
        body,
        mesh=mesh,
        in_specs=(
            P("tm", "panel", None),
            P("tm", None, "panel"),
            P("tm", "panel", None),
            P("tm", "panel", None),
            P("tm", "panel", None),
            P("tm", "panel", None),
            P("tm", "panel"),
        ),
        out_specs=(P("tm", "panel", None), P("tm", "panel", None), P("tm", "panel", None)),
        check_vma=False,
    )
```

```python
import jax
import jax.numpy as jnp
from jax import lax
from jax.experimental import pallas as pl
from jax.experimental.pallas import tpu as pltpu
from jax.sharding import PartitionSpec as P

MESH = pl.DeviceIdType.MESH
ROWS = 64
N = 1024
KEYS = (
    "a_R", "a_L", "b_Y",
    "fa_R", "fa_L", "ya_0", "ya_L", "ya_R", "b_R", "b_L", "pb_R", "pb_L",
    "fb_R", "fpb_R", "fb_L", "fpb_L", "ya_2",
    "sib_0", "sib_x", "sib_l", "sib_r", "sib_o",
)
NKEYS = len(KEYS)
SWAP0 = 4 * NKEYS
RET0 = SWAP0 + 5
NSEM = RET0 + 10
SPLIT = ((32, 16, 16), (32, 16, 16), (32, 16, 16), (16, 16, 16))


SEQ = (('s1', 0), ('s1', 1), ('s1', 2), ('o2', 0), ('s2', 0), ('s1', 3), ('o2', 1), ('s2', 1), ('s3', 0), ('o2', 2), ('s2', 2), ('o2', 3), ('s3', 1), ('s2', 3), ('s4a', 0), ('s4b', 0), ('c0', 0), ('c0', 1), ('s3', 2), ('s4a', 1), ('s4b', 1), ('c1', 0), ('c1', 1), ('s3', 3), ('s4a', 2), ('s4b', 2), ('c2', 0), ('c2', 1))


def nt(left, right):
    return lax.dot_general(left, right, (((1,), (1,)), ((), ())), preferred_element_type=jnp.float32)


def nn(left, right):
    return jnp.dot(left, right, preferred_element_type=jnp.float32)


def kernel(
    kept_ref, cin_ref, cout_ref, w_ref, sk_ref, s_ref, obs_ref,
    block_ref, coup_ref, src_ref,
    fw, fs, fo, fi, keptv, skv, obsv, cc, xt, vacc, vb, r45,
    send13, send4, send2, send5, recv13, recv4, recv2, recv5,
    ssem, rsem, lsem, ready,
):
    kept_n = lax.axis_size("tm")
    k = lax.axis_index("tm")
    panel = lax.axis_index("panel")
    x, y = lax.rem(panel, 4), panel // 4
    core = lax.rem(k, 2)
    half = y // 2
    home = core == half
    guest = core != half
    py = jnp.where(home, y, 3 - y)
    pyq = py + 1 - 2 * lax.rem(py, 2)
    job = k - core + half
    mine = py * 4 + x

    right = {"panel": y * 4 + lax.rem(x + 1, 4)}
    left = {"panel": y * 4 + lax.rem(x + 3, 4)}
    across = {"panel": (y + 1 - 2 * lax.rem(y, 2)) * 4 + x}
    sibling = {"tm": k + 1 - 2 * core}
    partner = {"tm": k + 1 - 2 * core, "panel": (3 - y) * 4 + x}
    follower = {"tm": lax.rem(job + 1, kept_n), "panel": mine}
    has_follower = job + 1 < kept_n
    has_leader = k > 0
    before = jnp.maximum(k - 1, 0)
    before_core = lax.rem(before, 2)
    before_home = before_core == half
    leader = {
        "tm": jnp.where(before_home, before, before + 1 - 2 * before_core),
        "panel": jnp.where(before_home, panel, (3 - y) * 4 + x),
    }

    load_kept = pltpu.make_async_copy(kept_ref.at[0], keptv, lsem.at[0])
    load_sk = pltpu.make_async_copy(sk_ref.at[0], skv, lsem.at[1])
    load_obs = pltpu.make_async_copy(obs_ref, obsv, lsem.at[2])

    barrier = pltpu.get_barrier_semaphore()
    for peer in (right, left, across, sibling):
        pl.semaphore_signal(barrier, inc=1, device_id=peer, device_id_type=MESH)

    @pl.when(guest)
    def _():
        pl.semaphore_signal(barrier, inc=1, device_id=partner, device_id_type=MESH)

    @pl.when(has_follower)
    def _():
        pl.semaphore_signal(barrier, inc=1, device_id=follower, device_id_type=MESH)

    full = (fw, fs, fo, fi)
    own = (w_ref.at[0], s_ref.at[0], cout_ref.at[0], cin_ref.at[0])

    def rows(m, p, r0, n):
        return full[m].at[pl.ds(pl.multiple_of(p * ROWS + r0, 16), n)]

    def home_copy(m):
        return pltpu.make_async_copy(own[m], rows(m, panel, 0, ROWS), lsem.at[3 + m])

    def guest_copies(m):
        a = SPLIT[0][0] if m == 0 else ROWS
        pieces = ((0, a, SWAP0 + m), (a, ROWS - a, SWAP0 + 4))
        return [
            pltpu.make_async_remote_copy(
                src_ref=own[m].at[pl.ds(r0, n)], dst_ref=rows(m, panel, r0, n),
                send_sem=ssem.at[at], recv_sem=rsem.at[at],
                device_id=partner, device_id_type=MESH,
            )
            for r0, n, at in pieces
            if n
        ]

    @pl.when(home)
    def _():
        for m in range(4):
            home_copy(m).start()

    load_kept.start()
    load_sk.start()
    load_obs.start()

    @pl.when(k == 0)
    def _():
        recv2[...] = jnp.zeros_like(recv2)
        recv5[...] = jnp.zeros_like(recv5)

    pl.semaphore_wait(barrier, 4 + guest.astype(jnp.int32) + has_leader.astype(jnp.int32))

    @pl.when(guest)
    def _():
        for m in range(4):
            for copy in guest_copies(m):
                copy.start()

    @pl.when(has_leader)
    def _():
        pl.semaphore_signal(ready, inc=1, device_id=leader, device_id_type=MESH)

    def swapped(m, i=0):
        if i == 0:

            @pl.when(home)
            def _():
                home_copy(m).wait()

        if i < len(guest_copies(m)):

            @pl.when(guest)
            def _():
                guest_copies(m)[i].wait_recv()

    copies = {}

    def send(m, key, p, r0, n, peer, start=True):
        if n == 0:
            return
        at = m * NKEYS + KEYS.index(key)
        copy = pltpu.make_async_remote_copy(
            src_ref=rows(m, p, r0, n), dst_ref=rows(m, p, r0, n),
            send_sem=ssem.at[at], recv_sem=rsem.at[at],
            device_id=peer, device_id_type=MESH,
        )
        if start:
            copy.start()
        copies[m, key] = copy

    def got(m, *keys):
        for key in keys:
            if (m, key) in copies:
                copies[m, key].wait_recv()

    xl, xr, xo = lax.rem(x + 3, 4), lax.rem(x + 1, 4), lax.rem(x + 2, 4)
    row, rowq = py * 4, pyq * 4

    def s1(m):
        a = SPLIT[m][0]
        swapped(m)
        send(m, "a_R", mine, 0, a, right)
        send(m, "a_L", mine, 0, a, left)
        swapped(m, 1)
        send(m, "b_Y", mine, a, ROWS - a, across)

    def o2(m):
        a = SPLIT[m][0]
        send(m, "ya_0", mine, 0, a, across)
        send(m, "b_R", mine, a, ROWS - a, right)
        send(m, "b_L", mine, a, ROWS - a, left)

    def s2(m):
        a, ra, _ = SPLIT[m]
        got(m, "a_R")
        send(m, "fa_R", row + xl, 0, ra, right)
        got(m, "a_L")
        send(m, "fa_L", row + xr, ra, a - ra, left)
        send(m, "ya_L", row + xl, 0, a, across)
        send(m, "ya_R", row + xr, 0, a, across)
        got(m, "b_Y")
        send(m, "pb_R", rowq + x, a, ROWS - a, right)
        send(m, "pb_L", rowq + x, a, ROWS - a, left)

    def s3(m):
        a, _, rb = SPLIT[m]
        got(m, "fa_R", "fa_L")
        send(m, "ya_2", row + xo, 0, a, across)
        got(m, "b_R")
        send(m, "fb_R", row + xl, a, rb, right)
        got(m, "b_L")
        send(m, "fb_L", row + xr, a + rb, ROWS - a - rb, left)
        got(m, "pb_R")
        send(m, "fpb_R", rowq + xl, a, rb, right)
        got(m, "pb_L")
        send(m, "fpb_L", rowq + xr, a + rb, ROWS - a - rb, left)

    def s4a(m):
        got(m, "fb_R", "fb_L")
        send(m, "sib_0", row, 0, 4 * ROWS, sibling)

    def s4b(m):
        got(m, "ya_0")
        send(m, "sib_x", rowq + x, 0, ROWS, sibling)
        got(m, "ya_L")
        send(m, "sib_l", rowq + xl, 0, ROWS, sibling)
        got(m, "ya_R")
        send(m, "sib_r", rowq + xr, 0, ROWS, sibling)
        got(m, "fpb_R", "fpb_L", "ya_2")
        send(m, "sib_o", rowq + xo, 0, ROWS, sibling)

    def back(at, src, dst, peer):
        return pltpu.make_async_remote_copy(
            src_ref=src, dst_ref=dst, send_sem=ssem.at[RET0 + at], recv_sem=rsem.at[RET0 + at],
            device_id=peer, device_id_type=MESH,
        )

    def span(p):
        return pl.ds(pl.multiple_of(p * 256, 256), 256)

    spans = [span(p) for p in (py, pyq, 3 - py, 3 - pyq)]
    groups = [span(p) for p in (py, 3 - py, jnp.where(home, pyq, 3 - pyq), jnp.where(home, 3 - pyq, pyq))]
    theirs = [span(p) for p in (3 - py, py, pyq, 3 - pyq)]
    ret4 = back(0, send4, recv4, partner)
    ret5 = back(1, send5, recv5, follower)
    ret13 = [back(2 + i, send13.at[:, groups[i]], recv13.at[:, groups[i]], partner) for i in range(4)]
    ret2 = [back(6 + i, send2.at[:, spans[i]], recv2.at[:, spans[i]], follower) for i in range(4)]

    def need(m, i):
        if i == 2:
            got(m, "sib_0")
        if i == 3:
            got(m, "sib_x", "sib_l", "sib_r", "sib_o")

    def c0(half_of):
        if half_of == 0:
            cc[0:ROWS, :] = fi[pl.ds(pl.multiple_of(mine * ROWS, ROWS), ROWS), :]
            cc[ROWS:, :] = fo[pl.ds(pl.multiple_of(mine * ROWS, ROWS), ROWS), :]
        for i in (2 * half_of, 2 * half_of + 1):
            need(0, i)
            part = fw[spans[i], :]
            xt[...] = nt(cc[...], part).astype(jnp.bfloat16)
            if i == 0:
                vacc[...] = nn(xt[...], part)
            else:
                vacc[...] += nn(xt[...], part)
        if half_of == 1:
            vb[...] = vacc[...].astype(jnp.bfloat16)

    def c1(half_of):
        for i in (2 * half_of, 2 * half_of + 1):
            need(1, i)
            part = nn(vb[:, spans[i]], fs[spans[i], :])
            if i == 0:
                r45[...] = part
            else:
                r45[...] += part
        if half_of == 0:
            return
        send5[...] = r45[ROWS:, :].astype(jnp.bfloat16)

        @pl.when(has_follower)
        def _():
            pl.semaphore_wait(ready, 1)
            ret5.start()

        @pl.when(guest)
        def _():
            send4[...] = r45[:ROWS, :].astype(jnp.bfloat16)
            ret4.start()

    def c2(half_of):
        for i in (2 * half_of, 2 * half_of + 1):
            need(2, i)
            send2[:, spans[i]] = nt(vb[ROWS:, :], fo[spans[i], :]).astype(jnp.bfloat16)

            @pl.when(has_follower)
            def _():
                ret2[i].start()

    steps = {"s1": s1, "o2": o2, "s2": s2, "s3": s3, "s4a": s4a, "s4b": s4b, "c0": c0, "c1": c1, "c2": c2}
    for step, m in SEQ:
        steps[step](m)

    def stay(i):
        both = nt(vb[...], fi[groups[i], :])
        block_ref[0, :, groups[i]] = -both[:ROWS, :]
        coup_ref[0, :, groups[i]] = -both[ROWS:, :]

    def give(i):
        send13[:, groups[i]] = nt(vb[...], fi[groups[i], :]).astype(jnp.bfloat16)
        ret13[i].start()

    def c3(i):
        @pl.when(home)
        def _():
            stay(i)

        @pl.when(guest)
        def _():
            give(i)

    s4a(3)
    c3(0)
    got(3, "ya_0")
    send(3, "sib_x", rowq + x, 0, ROWS, sibling)
    got(3, "ya_L")
    send(3, "sib_l", rowq + xl, 0, ROWS, sibling)
    got(3, "ya_R")
    send(3, "sib_r", rowq + xr, 0, ROWS, sibling)
    got(3, "sib_0")
    c3(1)
    send(3, "sib_o", rowq + xo, 0, ROWS, sibling, False)
    last = ("fpb_R", "fpb_L", "ya_2")
    others = ("sib_x", "sib_l", "sib_r", "sib_o")

    @pl.when(home)
    def _():
        got(3, *last)
        copies[3, "sib_o"].start()
        stay(2)

    @pl.when(guest)
    def _():
        got(3, *others)
        give(2)
        got(3, *last)
        copies[3, "sib_o"].start()
        give(3)

    load_kept.wait()
    load_sk.wait()
    load_obs.wait()
    at = pl.ds(pl.multiple_of(panel // 2 * 128, 128), 128)
    twice = 2.0 * obsv[...].astype(jnp.float32)
    twice = jnp.concatenate([twice, twice], axis=1)
    on = lax.broadcasted_iota(jnp.int32, (ROWS, 128), 1) == (
        lax.broadcasted_iota(jnp.int32, (ROWS, 128), 0) + ROWS * lax.rem(panel, 2)
    )
    keptv[:, at] = keptv[:, at] + jnp.where(on, jnp.broadcast_to(twice, (ROWS, 128)), 0.0)

    @pl.when(has_leader)
    def _():
        ret5.wait_recv()

    @pl.when(home)
    def _():
        src_ref[0] = skv[...].astype(jnp.float32) - recv5[...].astype(jnp.float32) - r45[:ROWS, :]

    @pl.when(guest)
    def _():
        ret4.wait_recv()
        src_ref[0] = skv[...].astype(jnp.float32) - recv5[...].astype(jnp.float32) - recv4[...].astype(jnp.float32)

    @pl.when(home)
    def _():
        got(3, *others)
        stay(3)

    for copy in copies.values():
        copy.wait_send()

    @pl.when(has_leader)
    def _():
        for i in range(4):
            ret2[i].wait_recv()

    keptv[...] = keptv[...] - recv2[...].astype(jnp.float32)

    @pl.when(home)
    def _():
        block_ref[0] = keptv[...] + block_ref[0]

    @pl.when(guest)
    def _():
        for m in range(4):
            for copy in guest_copies(m):
                copy.wait_send()
        ret4.wait_send()
        for i in range(4):
            ret13[i].wait_recv()
            block_ref[0, :, theirs[i]] = keptv[:, theirs[i]] - recv13[:ROWS, theirs[i]].astype(jnp.float32)
            coup_ref[0, :, theirs[i]] = -recv13[ROWS:, theirs[i]].astype(jnp.float32)
        for i in range(4):
            ret13[i].wait_send()

    @pl.when(has_follower)
    def _():
        ret5.wait_send()
        for i in range(4):
            ret2[i].wait_send()


def store(*refs):
    ins, outs, sem = refs[:3], refs[3:6], refs[6]
    puts = [pltpu.make_async_copy(ins[i], outs[i], sem.at[i]) for i in range(3)]
    for copy in puts:
        copy.start()
    for copy in puts:
        copy.wait()


def body(kept_block, coupling_in, *rest):
    args = (kept_block, jnp.swapaxes(coupling_in, 1, 2), *rest)
    args = tuple(pltpu.with_memory_space_constraint(a, pltpu.HBM) for a in args)
    bf16, f32 = jnp.bfloat16, jnp.float32
    vmem = pltpu.VMEM
    wide = lambda rows, dtype: vmem((rows, N), dtype)
    shapes = tuple(jax.ShapeDtypeStruct((1, ROWS, N), f32) for _ in range(3))
    results = pl.pallas_call(
        kernel,
        out_shape=shapes,
        in_specs=[pl.BlockSpec(memory_space=pltpu.HBM)] * 7,
        out_specs=(pl.BlockSpec(memory_space=pltpu.VMEM),) * 3,
        scratch_shapes=[wide(N, bf16)] * 4
        + [wide(ROWS, f32), wide(ROWS, bf16), vmem((1, ROWS), jnp.int32)]
        + [wide(2 * ROWS, bf16), vmem((2 * ROWS, 256), bf16), wide(2 * ROWS, f32), wide(2 * ROWS, bf16)]
        + [wide(2 * ROWS, f32)]
        + [wide(2 * ROWS, bf16)] + [wide(ROWS, bf16)] * 3 + [wide(2 * ROWS, bf16)] + [wide(ROWS, bf16)] * 3
        + [pltpu.SemaphoreType.DMA((NSEM,))] * 2
        + [pltpu.SemaphoreType.DMA((16,)), pltpu.SemaphoreType.REGULAR],
        compiler_params=pltpu.CompilerParams(
            collective_id=0, has_side_effects=True, vmem_limit_bytes=40 << 20
        ),
    )(*args)
    return pl.pallas_call(
        store,
        out_shape=shapes,
        in_specs=[pl.BlockSpec(memory_space=pl.ANY)] * 3,
        out_specs=(pl.BlockSpec(memory_space=pltpu.HBM),) * 3,
        scratch_shapes=[pltpu.SemaphoreType.DMA((3,))],
        compiler_params=pltpu.CompilerParams(vmem_limit_bytes=16 << 20),
    )(*results)


def solution(mesh):
    return jax.shard_map(
        body,
        mesh=mesh,
        in_specs=(
            P("tm", "panel", None),
            P("tm", None, "panel"),
            P("tm", "panel", None),
            P("tm", "panel", None),
            P("tm", "panel", None),
            P("tm", "panel", None),
            P("tm", "panel"),
        ),
        out_specs=(P("tm", "panel", None), P("tm", "panel", None), P("tm", "panel", None)),
        check_vma=False,
    )
```
